128 devices in a mesh: row: 8 (over x_hi, y), col: 16 (over x_lo, z, core).
Axes of the slice: x: 4 (x_hi: 2, x_lo: 2; x = x_hi * 2 + x_lo), y: 4, z: 4, core: 2. Of those that a mesh axis runs over, the one named last changes fastest.
Arguments:
- features: bfloat16 [131072, 128], P(('col', 'row')), may hold values from -6 to 6
- weight: bfloat16 [128, 256], replicated, may hold values from -0.5 to 0.5
- bias: float32 [256], replicated, may hold values from -4 to 4
- adjacency: bfloat16 [8, 16, 256, 128, 128], P('row', 'col'), may hold values from -0.09375 to 0.09375
- block_rows: int32 [8, 16, 256], P('row', 'col'), may hold values from 0 to 127, as said below
- block_cols: int32 [8, 16, 256], P('row', 'col'), may hold values from 0 to 63, as said below
- block_count: int32 [8, 16], P('row', 'col'), may hold values from 128 to 256, as said below
- cotangent: bfloat16 [131072, 256], P(('row', 'col')), may hold values from -6 to 6
- relu_mask: int32 [131072, 256], P(('row', 'col')), may hold values 0 or 1
Outputs:
- output: bfloat16 [131072, 256], P(('row', 'col'))
- grad_features: bfloat16 [131072, 128], P(('col', 'row'))
- grad_weight: float32 [128, 256], replicated
- grad_bias: float32 [256], replicated
The draws below stay inside these ranges and needn't reach their ends.
Inputs may be any that keep to these rules, and one draw needn't show every extreme that they name: Each device's block_rows lie in 0 to 1024 * 16 / 128 - 1; the (row, col) pairs of one device's slots are distinct. Each device's block_cols lie in 0 to 1024 * 8 / 128 - 1; see block_rows. `block_count`: slots at or past a device's count hold values that are not part of A; some device has all 256 slots live.
All inputs are finite; a program needn't handle non-finite values. No bound on the sum of `relu_mask` on one device may be relied on, other than what follows from the above.
Results may differ from the reference program's by a relative error of at most 0.0049.
Values may be sent and summed in bfloat16 or wider, within the bound.
A program may use at most 192 MiB of HBM per device.

```python
import jax
import jax.numpy as jnp
from jax import lax

BLK = 128
F_IN = 128
HID = 256
NODE_DEV = 1024
KB = 256
NODES = 131072
N_ROW = 8
N_COL = 16


def slot_positions(key):
    count_dev = N_ROW * N_COL
    places = NODE_DEV * N_COL // BLK * (NODE_DEV * N_ROW // BLK)
    keys = jax.random.split(key, count_dev)

    def one_device(single):
        first_key, second_key = jax.random.split(single)
        inner = jax.random.permutation(first_key, places - 2)[:KB - 2] + 1
        ends = jnp.array([0, places - 1], dtype=jnp.int32)
        listed = jnp.concatenate([ends, inner.astype(jnp.int32)])
        order = jax.random.permutation(second_key, KB)
        return listed[order]
    chosen = jax.vmap(one_device)(keys)
    return chosen.astype(jnp.int32)


def draw_block_rows(key, part):
    chosen = slot_positions(key)
    width_cols = NODE_DEV * N_ROW // BLK
    return (chosen // width_cols).reshape(N_ROW, N_COL, KB).astype(jnp.int32)


def draw_block_cols(key, part):
    chosen = slot_positions(key)
    width_cols = NODE_DEV * N_ROW // BLK
    return (chosen % width_cols).reshape(N_ROW, N_COL, KB).astype(jnp.int32)


def draw_block_count(key, part):
    key = jax.random.fold_in(key, 7)
    first_key, second_key = jax.random.split(key)
    counts = jax.random.randint(first_key, (N_ROW * N_COL,), KB // 2, KB + 1).astype(jnp.int32)
    fullest = jax.random.randint(second_key, (), 0, N_ROW * N_COL)
    counts = counts.at[fullest].set(KB)
    return counts.reshape(N_ROW, N_COL).astype(jnp.int32)


def touch_ends(values, stream_key, low, high):
    dims = values.shape
    index_at = [jax.random.randint(jax.random.fold_in(stream_key, axis), (), 0, dims[axis]) for axis in range(len(dims))]
    values = values.at[tuple(index_at)].set(low)
    longest = dims.index(max(dims))
    index_at[longest] = (index_at[longest] + 1) % dims[longest]
    return values.at[tuple(index_at)].set(high)


def shard_levels(key, extent, pieces, low, top_value):
    def one(dim, blocks):
        draws = jax.random.uniform(jax.random.fold_in(jax.random.fold_in(key, 6), dim), (blocks,), jnp.float32, low / len(pieces), top_value / len(pieces))
        return jnp.repeat(jnp.exp(draws), extent[dim] // blocks).reshape((-1,) + (1,) * (len(extent) - dim - 1))

    factor_of = one(*pieces[0])
    for cut in pieces[1:]:
        factor_of = factor_of * one(*cut)
    return factor_of


def gaussian(rng, dims, width, most, shards=(), kind=jnp.bfloat16):
    values = width * jax.random.normal(rng, dims, jnp.float32)
    if shards:
        values = values * shard_levels(rng, dims, shards, -0.22, 0.18)
    return jnp.clip(values, -most, most).astype(kind)


def setup_inputs(seed: int = 0) -> dict:
    splits = jax.random.split(jax.random.key(seed), 10)
    return {
        "features": gaussian(splits[0], (NODES, F_IN), 1.0, 6.0, ((0, 128),)),
        "weight": gaussian(splits[1], (F_IN, HID), F_IN ** -0.5, 0.5),
        "bias": gaussian(splits[2], (HID,), 1.0, 4.0, (), jnp.float32),
        "adjacency": gaussian(splits[3], (N_ROW, N_COL, KB, BLK, BLK), (BLK * BLK * KB // NODE_DEV) ** -0.5, 0.09375, ((0, 8), (1, 16))),
        "block_rows": draw_block_rows(jax.random.fold_in(splits[9], 71), 0),
        "block_cols": draw_block_cols(jax.random.fold_in(splits[9], 71), 0),
        "block_count": draw_block_count(jax.random.fold_in(splits[9], 71), 0),
        "cotangent": gaussian(splits[7], (NODES, HID), 1.0, 6.0, ((0, 128),)),
        "relu_mask": touch_ends((jax.random.randint(splits[8], (NODES, HID), 0, 2) < 1).astype(jnp.int32), jax.random.fold_in(splits[8], 1), 0, 1),
    }


def reference(features, weight, bias, adjacency, block_rows, block_cols, block_count, cotangent, relu_mask):
    devs = N_ROW * N_COL
    row_blocks = NODE_DEV * N_COL // BLK
    col_blocks = NODE_DEV * N_ROW // BLK
    total_blocks = NODES // BLK
    flat_adj = adjacency.reshape(devs, KB, BLK, BLK)
    flat_rows = block_rows.reshape(devs, KB)
    flat_cols = block_cols.reshape(devs, KB)
    flat_count = block_count.reshape(devs)
    slot_ids = jnp.arange(KB, dtype=jnp.int32)

    def coords(index):
        global_rows = (index // N_COL) * row_blocks + flat_rows[index]
        global_cols = (index % N_COL) * col_blocks + flat_cols[index]
        alive = (slot_ids < flat_count[index]).astype(jnp.float32)
        return global_rows.astype(jnp.int32), global_cols.astype(jnp.int32), alive

    feat_blocks = features.reshape(total_blocks, BLK, F_IN)

    def forward_step(carry, index):
        global_rows, global_cols, alive = coords(index)
        blocks = flat_adj[index].astype(jnp.float32)
        picked = feat_blocks[global_cols].astype(jnp.float32)
        products = jnp.einsum("kab,kbf->kaf", blocks, picked) * alive[:, None, None]
        return carry + jax.ops.segment_sum(products, global_rows, num_segments=total_blocks), None

    start = jnp.zeros((total_blocks, BLK, F_IN), jnp.float32)
    summed, _ = lax.scan(forward_step, start, jnp.arange(devs, dtype=jnp.int32))
    aggregated = summed.reshape(NODES, F_IN).astype(jnp.bfloat16)
    mask_float = relu_mask.astype(jnp.float32)
    preact = jnp.dot(aggregated, weight, preferred_element_type=jnp.float32) + bias
    output = (preact * mask_float).astype(jnp.bfloat16)
    grad_pre = (cotangent.astype(jnp.float32) * mask_float).astype(jnp.bfloat16)
    grad_weight = jnp.dot(aggregated.T, grad_pre, preferred_element_type=jnp.float32)
    grad_bias = jnp.sum(grad_pre.astype(jnp.float32), axis=0)
    grad_proj = jnp.dot(grad_pre, weight.T, preferred_element_type=jnp.float32).astype(jnp.bfloat16)
    proj_blocks = grad_proj.reshape(total_blocks, BLK, F_IN)

    def backward_step(carry, index):
        global_rows, global_cols, alive = coords(index)
        blocks = flat_adj[index].astype(jnp.float32)
        picked = proj_blocks[global_rows].astype(jnp.float32)
        products = jnp.einsum("kab,kaf->kbf", blocks, picked) * alive[:, None, None]
        return carry + jax.ops.segment_sum(products, global_cols, num_segments=total_blocks), None

    summed_back, _ = lax.scan(backward_step, start, jnp.arange(devs, dtype=jnp.int32))
    grad_features = summed_back.reshape(NODES, F_IN).astype(jnp.bfloat16)
    return output, grad_features, grad_weight, grad_bias
```

```python
import functools

import jax
import jax.numpy as jnp
from jax import lax
from jax.experimental import pallas as pl
from jax.experimental.pallas import tpu as pltpu
from jax.sharding import PartitionSpec as P

F32 = jnp.float32
BF16 = jnp.bfloat16
MESH = pl.DeviceIdType.MESH
BLK = 128
SHARD = 8
HALF = 4


def plan_kernel(count_ref, rows_ref, cols_ref, idx_ref, flt_ref):
    n = rows_ref.shape[1]
    count = count_ref[0, 0]
    lane = lax.broadcasted_iota(jnp.int32, (n, n), 1)
    sub = lax.broadcasted_iota(jnp.int32, (n, n), 0)
    lane_f, sub_f = lane.astype(F32), sub.astype(F32)
    eye = lane == sub
    live_l, live_c = lane < count, sub < count
    row_l = jnp.broadcast_to(rows_ref[...].astype(F32), (n, n))
    col_l = jnp.broadcast_to(cols_ref[...].astype(F32), (n, n))
    zero = jnp.zeros((n, n), F32)
    row_c = jnp.broadcast_to(jnp.sum(jnp.where(eye, row_l, zero), axis=1, keepdims=True), (n, n))
    col_c = jnp.broadcast_to(jnp.sum(jnp.where(eye, col_l, zero), axis=1, keepdims=True), (n, n))
    idx_ref[...] = jnp.zeros_like(idx_ref)
    flt_ref[...] = jnp.zeros_like(flt_ref)
    one = jnp.ones((n, n), F32)
    for side, (major_l, major_c, minor_c) in enumerate(((row_l, row_c, col_c), (col_l, col_c, row_c))):
        far = jnp.full((n, n), 65536.0, F32)
        key_l = jnp.where(live_l, major_l * n, far) + lane_f
        key_c = jnp.where(live_c, major_c * n, far) + sub_f
        rank = jnp.sum(jnp.where(key_l < key_c, one, zero), axis=1, keepdims=True)
        hot = jnp.where(jnp.broadcast_to(rank, (n, n)) == lane_f, one, zero)
        same = jnp.where(major_l == major_c, one, zero) * jnp.where(lane < sub, one, zero) * jnp.where(live_l, one, zero)
        keep = jnp.where(jnp.sum(same, axis=1, keepdims=True) > 0.5, 1.0, 0.0)
        slot = jnp.sum(hot * sub_f, axis=0, keepdims=True)
        minor = jnp.sum(hot * minor_c, axis=0, keepdims=True)
        keep_sorted = jnp.sum(hot * keep, axis=0, keepdims=True)
        live_f = jnp.where(live_c, one, zero)
        upto = jnp.sum(jnp.where(major_c <= lane_f, live_f, zero), axis=0, keepdims=True)
        here = jnp.sum(jnp.where(major_c == lane_f, live_f, zero), axis=0, keepdims=True)
        idx_ref[3 * side : 3 * side + 1, :] = slot.astype(jnp.int32)
        idx_ref[3 * side + 1 : 3 * side + 2, :] = minor.astype(jnp.int32)
        idx_ref[3 * side + 2 : 3 * side + 3, :] = jnp.maximum(upto - 1.0, 0.0).astype(jnp.int32)
        flt_ref[2 * side : 2 * side + 1, :] = keep_sorted
        flt_ref[2 * side + 1 : 2 * side + 2, :] = jnp.where(here > 0.5, 1.0, 0.0)


class Lines:
    def __init__(self, send_sems, recv_sems):
        self.send_sems, self.recv_sems, self.used, self.sent = send_sems, recv_sems, 0, []

    def line(self):
        self.used += 1
        return self.used - 1

    def send(self, line, src, dst, device):
        copy = pltpu.make_async_remote_copy(
            src_ref=src, dst_ref=dst, send_sem=self.send_sems.at[line], recv_sem=self.recv_sems.at[line],
            device_id=device, device_id_type=MESH)
        copy.start()
        self.sent.append(copy)

    def wait(self, line, dst, device):
        pltpu.make_async_remote_copy(
            src_ref=dst, dst_ref=dst, send_sem=self.send_sems.at[line], recv_sem=self.recv_sems.at[line],
            device_id=device, device_id_type=MESH).wait_recv()

    def drain(self):
        for copy in self.sent:
            copy.wait_send()


N_LINES = 160


def layer_kernel(
    idx_ref, flt_ref, feat_ref, weight_ref, bias_ref, cot_ref, mask_ref, adj_ref,
    out_ref, gf_ref, gw_ref, gb_ref,
    adj, run, feats, proj, gpre, rsend, crecv, rown,
    zs1, zr1, zs2, zr2, zxs, zxr, ys1, yr1, ys2, yr2, yxs, yxr,
    agg, gsum, ar_core, ar_z, ar_y, ar_x, gall,
    send_sems, recv_sems, adj_sem):
    row, col = lax.axis_index("row"), lax.axis_index("col")
    xh, y = row // 4, row % 4
    xl, z, core = col // 8, (col // 2) % 4, col % 2
    lines = Lines(send_sems, recv_sems)

    def dev(xh=xh, y=y, xl=xl, z=z, core=core):
        return (xh * 4 + y, (xl * 4 + z) * 2 + core)

    def at_y(step):
        return dev(y=(y + step) % 4)

    def at_z(step):
        return dev(z=(z + step) % 4)

    pair_x = dev(xh=1 - xh)
    near_x = dev(xl=1 - xl)
    diag_x = dev(xh=1 - xh, xl=1 - xl)
    other = dev(core=1 - core)
    partners = [at_y(1), at_y(2), at_y(3), at_z(1), at_z(2), at_z(3), pair_x, near_x, diag_x, other]

    adj_copy = pltpu.make_async_copy(adj_ref, adj, adj_sem)
    adj_copy.start()

    barrier = pltpu.get_barrier_semaphore()
    for partner in partners:
        pl.semaphore_signal(barrier, inc=1, device_id=partner, device_id_type=MESH)
    pl.semaphore_wait(barrier, len(partners))

    def part(buf, shard, half):
        return buf.at[pl.ds(shard * SHARD + half * HALF, HALF)]

    class Gather:
        def __init__(self, buf, own, shard, pos, pair, ring, mate):
            self.buf, self.own, self.shard, self.pos, self.pair, self.ring, self.mate = buf, own, shard, pos, pair, ring, mate
            self.l0 = [lines.line() for _ in range(2)]
            self.l1 = [[lines.line() for _ in range(2)] for _ in range(2)]
            self.l2 = [lines.line() for _ in range(2)]
            self.l3 = [[lines.line() for _ in range(2)] for _ in range(2)]
            self.l4 = [lines.line() for _ in range(2)]

        def place(self, pair_step, step, half):
            pair = self.pair if pair_step == 0 else 1 - self.pair
            return part(self.buf, self.shard(pair, (self.pos + step) % 4), half)

        def begin(self):
            for half in range(2):
                for d in range(2):
                    h = half if d == 0 else 1 - half
                    lines.send(self.l1[d][h], self.own(h), self.place(0, 0, h), self.ring(1 - 2 * d))
            for half in range(2):
                lines.send(self.l0[half], self.own(half), self.place(0, 0, half), self.mate)

        def got_mate(self, h):
            lines.wait(self.l0[h], self.place(1, 0, h), self.mate)
            return self.place(1, 0, h)

        def pass_mate(self, h):
            for d in range(2):
                lines.send(self.l3[d][h], self.place(1, 0, h), self.place(1, 0, h), self.ring(1 - 2 * d))

        def got_ring(self, kind, d, h):
            step = 2 * d - 1
            table = self.l1 if kind == 0 else self.l3
            place = self.place(kind, step, h)
            lines.wait(table[d][h], place, self.ring(step))
            return place

        def pass_ring(self, kind, d):
            step = 2 * d - 1
            table = self.l2 if kind == 0 else self.l4
            place = self.place(kind, step, d)
            lines.send(table[d], place, place, self.ring(-step))

        def got_far(self, kind, d):
            step = 2 * d - 1
            table = self.l2 if kind == 0 else self.l4
            place = self.place(kind, 2, d)
            lines.wait(table[d], place, self.ring(step))
            return place

    rows_g = Gather(feats, lambda h: feat_ref.at[pl.ds(h * HALF, HALF)],
                    lambda pair, pos: pair * 4 + pos, y, xh, at_y, pair_x)
    rows_g.begin()

    gb_ref[...] = jnp.zeros_like(gb_ref)

    def project(b, _):
        nodes = pl.ds(pl.multiple_of(b * BLK, BLK), BLK)
        grad = cot_ref[nodes, :].astype(F32) * mask_ref[nodes, :].astype(F32)
        grad16 = grad.astype(BF16)
        gpre[nodes, :] = grad16
        gb_ref[...] += jnp.sum(grad16.astype(F32), axis=0, keepdims=True)
        turned = lax.dot_general(weight_ref[...], grad16, (((1,), (1,)), ((), ())), preferred_element_type=F32)
        proj[col * SHARD + b] = turned.astype(BF16)
        return 0

    lax.fori_loop(0, SHARD, project, 0)
    cols_g = Gather(proj, lambda h: part(proj, col, h),
                    lambda pair, pos: (pair * 4 + pos) * 2 + core, z, xl, at_z, near_x)
    cols_g.begin()

    across = []

    def cross(pair_step, step, h):
        line = lines.line()
        place = cols_g.place(pair_step, step, h)
        lines.send(line, place, place, other)
        pair = xl if pair_step == 0 else 1 - xl
        there = part(proj, (pair * 4 + (z + step) % 4) * 2 + 1 - core, h)
        across.append((line, there))

    feats[pl.ds(row * SHARD, SHARD)] = feat_ref[...]

    cross(0, 0, 0)
    cross(0, 0, 1)
    for d in range(2):
        rows_g.got_ring(0, d, d)
        rows_g.pass_ring(0, d)
    for h in range(2):
        rows_g.got_mate(h)
        rows_g.pass_mate(h)
    for d in range(2):
        cols_g.got_ring(0, d, d)
        cols_g.pass_ring(0, d)
    for h in range(2):
        cols_g.got_mate(h)
        cols_g.pass_mate(h)
    for d in range(2):
        cross(0, 2 * d - 1, d)
    for h in range(2):
        cross(1, 0, h)
    for d in range(2):
        cols_g.got_ring(0, d, 1 - d)
        cross(0, 2 * d - 1, 1 - d)
    for d in range(2):
        rows_g.got_ring(1, d, d)
        rows_g.pass_ring(1, d)
    for d in range(2):
        cols_g.got_ring(1, d, d)
        cols_g.pass_ring(1, d)
        cross(1, 2 * d - 1, d)
    for d in range(2):
        cols_g.got_far(0, d)
        cross(0, 2, d)
    for d in range(2):
        cols_g.got_ring(1, d, 1 - d)
        cross(1, 2 * d - 1, 1 - d)
    for d in range(2):
        rows_g.got_ring(0, d, 1 - d)
        rows_g.got_far(0, d)
        rows_g.got_ring(1, d, 1 - d)
    for d in range(2):
        rows_g.got_far(1, d)
    for d in range(2):
        cols_g.got_far(1, d)
        cross(1, 2, d)
    adj_copy.wait()

    slots = adj.shape[0]

    def forward(p, total):
        total = total * flt_ref[0, p] + jnp.dot(adj[idx_ref[0, p]], feats[idx_ref[1, p]], preferred_element_type=F32)
        run[p] = total
        return total

    lax.fori_loop(0, slots, forward, jnp.zeros((BLK, BLK), F32), unroll=8)

    def row_block(b):
        return run[idx_ref[2, b]] * flt_ref[1, b]

    order = [(pair_step, step) for step in (2, 1, -1, 0) for pair_step in (1, 0)]

    def spot(pair, pos, step):
        return pair * 4 + (pos + step) % 4

    core_lines = {}
    for pair_step, step in order:
        q = spot(1 - xl if pair_step else xl, z, step)

        def fill(b, _, q=q):
            rsend[q * SHARD + b] = row_block((q * 2 + 1 - core) * SHARD + b).astype(BF16)
            return 0

        lax.fori_loop(0, SHARD, fill, 0)
        line = core_lines[pair_step, step] = lines.line()
        place = pl.ds(q * SHARD, SHARD)
        lines.send(line, rsend.at[place], crecv.at[place], other)

    def add_core(pair_step, step):
        q = spot(1 - xl if pair_step else xl, z, step)
        lines.wait(core_lines[pair_step, step], crecv.at[pl.ds(q * SHARD, SHARD)], other)

        def fill(b, _):
            rown[q * SHARD + b] = row_block((q * 2 + core) * SHARD + b) + crecv[q * SHARD + b].astype(F32)
            return 0

        lax.fori_loop(0, SHARD, fill, 0)

    class Scatter:
        def __init__(self, s1, r1, s2, r2, xs, xr, term, ring, mate):
            self.s1, self.r1, self.s2, self.r2, self.xs, self.xr = s1, r1, s2, r2, xs, xr
            self.term, self.ring, self.mate = term, ring, mate
            self.l1 = [[lines.line() for _ in range(2)] for _ in range(2)]
            self.l2 = [[[lines.line() for _ in range(2)] for _ in range(2)] for _ in range(2)]
            self.lx = [lines.line() for _ in range(2)]

        def far(self, pair_step):
            for d in range(2):
                def fill(b, _, d=d):
                    b = d * HALF + b
                    self.s1[pair_step * SHARD + b] = self.term(pair_step, 2, b).astype(BF16)
                    return 0

                lax.fori_loop(0, HALF, fill, 0)
                place = pl.ds(pair_step * SHARD + d * HALF, HALF)
                lines.send(self.l1[pair_step][d], self.s1.at[place], self.r1.at[place], self.ring(1 - 2 * d))

        def near(self, pair_step, d, late):
            h = d if late else 1 - d
            base = (pair_step * 2 + d) * SHARD + h * HALF
            if late:
                place = pl.ds(pair_step * SHARD + d * HALF, HALF)
                lines.wait(self.l1[pair_step][d], self.r1.at[place], self.ring(2 * d - 1))

            def fill(b, _):
                value = self.term(pair_step, 1 - 2 * d, h * HALF + b)
                if late:
                    value = value + self.r1[pair_step * SHARD + d * HALF + b].astype(F32)
                self.s2[base + b] = value.astype(BF16)
                return 0

            lax.fori_loop(0, HALF, fill, 0)
            place = pl.ds(base, HALF)
            lines.send(self.l2[pair_step][d][h], self.s2.at[place], self.r2.at[place], self.ring(1 - 2 * d))

        def wait_near(self, pair_step, h):
            for d in range(2):
                place = pl.ds((pair_step * 2 + d) * SHARD + h * HALF, HALF)
                lines.wait(self.l2[pair_step][d][h], self.r2.at[place], self.ring(2 * d - 1))

        def total(self, pair_step, b):
            base = pair_step * 2 * SHARD + b
            return (self.term(pair_step, 0, b) + self.r2[base].astype(F32)) + self.r2[base + SHARD].astype(F32)

        def swap(self, h):
            self.wait_near(1, h)

            def fill(b, _):
                self.xs[h * HALF + b] = self.total(1, h * HALF + b).astype(BF16)
                return 0

            lax.fori_loop(0, HALF, fill, 0)
            place = pl.ds(h * HALF, HALF)
            lines.send(self.lx[h], self.xs.at[place], self.xr.at[place], self.mate)

        def finish(self, h, use):
            self.wait_near(0, h)
            lines.wait(self.lx[h], self.xr.at[pl.ds(h * HALF, HALF)], self.mate)

            def body(b, _):
                b = h * HALF + b
                use(b, self.total(0, b) + self.xr[b].astype(F32))
                return 0

            lax.fori_loop(0, HALF, body, 0)

    def row_term(pair_step, step, b):
        return rown[spot(1 - xl if pair_step else xl, z, step) * SHARD + b]

    rows_s = Scatter(zs1, zr1, zs2, zr2, zxs, zxr, row_term, at_z, near_x)
    for pair_step in (1, 0):
        add_core(pair_step, 2)
        rows_s.far(pair_step)
    for pair_step in (1, 0):
        for d in range(2):
            add_core(pair_step, 1 - 2 * d)
            rows_s.near(pair_step, d, False)
    for pair_step in (1, 0):
        add_core(pair_step, 0)

    for line, there in across:
        lines.wait(line, there, other)

    def backward(p, total):
        total = total * flt_ref[2, p] + jnp.dot(proj[idx_ref[4, p]], adj[idx_ref[3, p]], preferred_element_type=F32)
        run[p] = total
        return total

    lax.fori_loop(0, slots, backward, jnp.zeros((BLK, BLK), F32), unroll=8)

    def col_term(pair_step, step, b):
        at = spot(1 - xh if pair_step else xh, y, step) * SHARD + b
        return run[idx_ref[5, at]] * flt_ref[3, at]

    cols_s = Scatter(ys1, yr1, ys2, yr2, yxs, yxr, col_term, at_y, pair_x)
    for pair_step in (1, 0):
        cols_s.far(pair_step)
    for pair_step in (1, 0):
        for d in range(2):
            cols_s.near(pair_step, d, False)
    for pair_step in (1, 0):
        for d in range(2):
            rows_s.near(pair_step, d, True)
    for h in range(2):
        rows_s.swap(h)
    for pair_step in (1, 0):
        for d in range(2):
            cols_s.near(pair_step, d, True)

    def layer(b, value):
        nodes = pl.ds(pl.multiple_of(b * BLK, BLK), BLK)
        sums = value.astype(BF16)
        agg[b] = sums
        pre = jnp.dot(sums, weight_ref[...], preferred_element_type=F32) + bias_ref[...]
        out_ref[nodes, :] = (pre * mask_ref[nodes, :].astype(F32)).astype(BF16)

    for h in range(2):
        rows_s.finish(h, layer)

    def weight_term(b, total):
        nodes = pl.ds(pl.multiple_of(b * BLK, BLK), BLK)
        return total + lax.dot_general(agg[b], gpre[nodes, :], (((0,), (0,)), ((), ())), preferred_element_type=F32)

    gw_ref[...] = lax.fori_loop(0, SHARD, weight_term, jnp.zeros(gw_ref.shape, F32))

    pieces = gsum.shape[0]
    depth = gw_ref.shape[0] // pieces
    for n in range(pieces):
        gsum[n, pl.ds(0, depth), :] = gw_ref[pl.ds(n * depth, depth), :]
        gsum[n, pl.ds(depth, 8), :] = jnp.broadcast_to(gb_ref[...], (8, gb_ref.shape[1]))
    line = lines.line()
    lines.send(line, gsum.at[pl.ds((1 - core) * 4, 4)], ar_core, other)
    for h in range(2):
        cols_s.swap(h)
    lines.wait(line, ar_core, other)
    for n in range(4):
        ar_core[n] = ar_core[n] + gsum[core * 4 + n]

    z_lines = [lines.line() for _ in range(3)]
    for step in (2, 1, 3):
        lines.send(z_lines[step - 1], ar_core.at[(z + step) % 4], ar_z.at[step], at_z(step))
    ar_z[0] = ar_core[z]
    for step in (1, 2, 3):
        lines.wait(z_lines[step - 1], ar_z.at[step], at_z(4 - step))
    ar_y[y] = (ar_z[0] + ar_z[1]) + (ar_z[2] + ar_z[3])
    y_lines = [lines.line() for _ in range(3)]
    for step in (2, 1, 3):
        lines.send(y_lines[step - 1], ar_y.at[y], ar_y.at[y], at_y(step))
    for step in (1, 2, 3):
        lines.wait(y_lines[step - 1], ar_y.at[(y + 4 - step) % 4], at_y(4 - step))
    x = xh * 2 + xl
    ar_x[x] = (ar_y[0] + ar_y[1]) + (ar_y[2] + ar_y[3])
    x_mates = [(near_x, xh * 2 + 1 - xl), (pair_x, (1 - xh) * 2 + xl), (diag_x, (1 - xh) * 2 + 1 - xl)]
    x_lines = [lines.line() for _ in range(3)]
    for line, (mate, _) in zip(x_lines, x_mates):
        lines.send(line, ar_x.at[x], ar_x.at[x], mate)
    for line, (mate, place) in zip(x_lines, x_mates):
        lines.wait(line, ar_x.at[place], mate)
    mine = core * 4 + z
    gall[mine] = (ar_x[0] + ar_x[1]) + (ar_x[2] + ar_x[3])
    e_lines = [lines.line() for _ in range(3)]
    for step in (2, 1, 3):
        lines.send(e_lines[step - 1], gall.at[mine], gall.at[mine], at_z(step))
    for step in (1, 2, 3):
        lines.wait(e_lines[step - 1], gall.at[core * 4 + (z + 4 - step) % 4], at_z(4 - step))
    line = lines.line()
    lines.send(line, gall.at[pl.ds(core * 4, 4)], gall.at[pl.ds(core * 4, 4)], other)

    def store(b, value):
        gf_ref[b] = jnp.transpose(value).astype(BF16)

    for h in range(2):
        cols_s.finish(h, store)

    lines.wait(line, gall.at[pl.ds((1 - core) * 4, 4)], other)
    for n in range(pieces):
        gw_ref[pl.ds(n * depth, depth), :] = gall[n, pl.ds(0, depth), :]
    gb_ref[...] = gall[0, pl.ds(depth, 1), :]
    lines.drain()
    assert lines.used <= N_LINES


def local(features, weight, bias, adjacency, block_rows, block_cols, block_count, cotangent, relu_mask):
    slots = adjacency.shape[2]
    vmem, smem, hbm = (pl.BlockSpec(memory_space=m) for m in (pltpu.VMEM, pltpu.SMEM, pl.ANY))
    idx, flt = pl.pallas_call(
        plan_kernel,
        out_shape=(jax.ShapeDtypeStruct((8, slots), jnp.int32), jax.ShapeDtypeStruct((8, slots), F32)),
        in_specs=[smem, vmem, vmem],
        out_specs=(vmem, vmem),
        name="plan",
    )(block_count, block_rows[0], block_cols[0])
    hid = weight.shape[1]

    def blocks(n, dtype=BF16):
        return pltpu.VMEM((n, BLK, BLK), dtype)

    scratch = [
        blocks(slots), blocks(slots, F32), blocks(64), blocks(128), pltpu.VMEM((1024, hid), BF16),
        blocks(64), blocks(64), blocks(64, F32)]
    for _ in range(2):
        scratch += [blocks(16), blocks(16), blocks(32), blocks(32), blocks(8), blocks(8)]
    piece = (24, hid)
    scratch += [blocks(8), pltpu.VMEM((8,) + piece, F32)]
    scratch += [pltpu.VMEM((4,) + piece, F32) for _ in range(4)] + [pltpu.VMEM((8,) + piece, F32)]
    scratch += [pltpu.SemaphoreType.DMA((N_LINES,)), pltpu.SemaphoreType.DMA((N_LINES,)), pltpu.SemaphoreType.DMA]
    out, gf, gw, gb = pl.pallas_call(
        layer_kernel,
        out_shape=(
            jax.ShapeDtypeStruct((1024, hid), BF16),
            jax.ShapeDtypeStruct((SHARD, BLK, BLK), BF16),
            jax.ShapeDtypeStruct(weight.shape, F32),
            jax.ShapeDtypeStruct((1, hid), F32),
        ),
        in_specs=[smem, smem, vmem, vmem, vmem, vmem, vmem, hbm],
        out_specs=(vmem, vmem, vmem, vmem),
        scratch_shapes=scratch,
        compiler_params=pltpu.CompilerParams(collective_id=0, has_side_effects=True, vmem_limit_bytes=60 * 2**20),
        name="layer",
    )(idx, flt, features.reshape(SHARD, BLK, BLK), weight, bias.reshape(1, hid), cotangent, relu_mask,
      adjacency.reshape(slots, BLK, BLK))
    return out, gf.reshape(1024, BLK), gw, gb.reshape(hid)


def solution(mesh):
    in_specs = (
        P(("col", "row"), None),
        P(),
        P(),
        P("row", "col", None, None, None),
        P("row", "col", None),
        P("row", "col", None),
        P("row", "col"),
        P(("row", "col"), None),
        P(("row", "col"), None),
    )
    out_specs = (P(("row", "col"), None), P(("col", "row"), None), P(), P())
    return jax.shard_map(local, mesh=mesh, in_specs=in_specs, out_specs=out_specs, check_vma=False)
```

```python
import functools

import jax
import jax.numpy as jnp
from jax import lax
from jax.experimental import pallas as pl
from jax.experimental.pallas import tpu as pltpu
from jax.sharding import PartitionSpec as P

F32 = jnp.float32
BF16 = jnp.bfloat16
MESH = pl.DeviceIdType.MESH
BLK = 128
SHARD = 8
HALF = 4


def plan_kernel(count_ref, rows_ref, cols_ref, idx_ref, flt_ref):
    n = rows_ref.shape[1]
    count = count_ref[0, 0]
    lane = lax.broadcasted_iota(jnp.int32, (n, n), 1)
    sub = lax.broadcasted_iota(jnp.int32, (n, n), 0)
    lane_f, sub_f = lane.astype(F32), sub.astype(F32)
    eye = lane == sub
    live_l, live_c = lane < count, sub < count
    row_l = jnp.broadcast_to(rows_ref[...].astype(F32), (n, n))
    col_l = jnp.broadcast_to(cols_ref[...].astype(F32), (n, n))
    zero = jnp.zeros((n, n), F32)
    row_c = jnp.broadcast_to(jnp.sum(jnp.where(eye, row_l, zero), axis=1, keepdims=True), (n, n))
    col_c = jnp.broadcast_to(jnp.sum(jnp.where(eye, col_l, zero), axis=1, keepdims=True), (n, n))
    idx_ref[...] = jnp.zeros_like(idx_ref)
    flt_ref[...] = jnp.zeros_like(flt_ref)
    one = jnp.ones((n, n), F32)
    for side, (major_l, major_c, minor_c) in enumerate(((row_l, row_c, col_c), (col_l, col_c, row_c))):
        far = jnp.full((n, n), 65536.0, F32)
        key_l = jnp.where(live_l, major_l * n, far) + lane_f
        key_c = jnp.where(live_c, major_c * n, far) + sub_f
        rank = jnp.sum(jnp.where(key_l < key_c, one, zero), axis=1, keepdims=True)
        hot = jnp.where(jnp.broadcast_to(rank, (n, n)) == lane_f, one, zero)
        same = jnp.where(major_l == major_c, one, zero) * jnp.where(lane < sub, one, zero) * jnp.where(live_l, one, zero)
        keep = jnp.where(jnp.sum(same, axis=1, keepdims=True) > 0.5, 1.0, 0.0)
        slot = jnp.sum(hot * sub_f, axis=0, keepdims=True)
        minor = jnp.sum(hot * minor_c, axis=0, keepdims=True)
        keep_sorted = jnp.sum(hot * keep, axis=0, keepdims=True)
        live_f = jnp.where(live_c, one, zero)
        upto = jnp.sum(jnp.where(major_c <= lane_f, live_f, zero), axis=0, keepdims=True)
        here = jnp.sum(jnp.where(major_c == lane_f, live_f, zero), axis=0, keepdims=True)
        idx_ref[3 * side : 3 * side + 1, :] = slot.astype(jnp.int32)
        idx_ref[3 * side + 1 : 3 * side + 2, :] = minor.astype(jnp.int32)
        idx_ref[3 * side + 2 : 3 * side + 3, :] = jnp.maximum(upto - 1.0, 0.0).astype(jnp.int32)
        flt_ref[2 * side : 2 * side + 1, :] = keep_sorted
        flt_ref[2 * side + 1 : 2 * side + 2, :] = jnp.where(here > 0.5, 1.0, 0.0)


def hand_on_kernel(*refs):
    half = len(refs) // 2
    for source, target in zip(refs[:half], refs[half:]):
        target[...] = source[...]


class Lines:
    def __init__(self, send_sems, recv_sems):
        self.send_sems, self.recv_sems, self.used, self.sent = send_sems, recv_sems, 0, []

    def line(self):
        self.used += 1
        return self.used - 1

    def send(self, line, src, dst, device):
        copy = pltpu.make_async_remote_copy(
            src_ref=src, dst_ref=dst, send_sem=self.send_sems.at[line], recv_sem=self.recv_sems.at[line],
            device_id=device, device_id_type=MESH)
        copy.start()
        self.sent.append(copy)

    def wait(self, line, dst, device):
        pltpu.make_async_remote_copy(
            src_ref=dst, dst_ref=dst, send_sem=self.send_sems.at[line], recv_sem=self.recv_sems.at[line],
            device_id=device, device_id_type=MESH).wait_recv()

    def drain(self):
        for copy in self.sent:
            copy.wait_send()


N_LINES = 160


def layer_kernel(
    idx_ref, flt_ref, feat_ref, weight_ref, bias_ref, cot_hbm, mask_hbm, adj_ref,
    out_ref, gf_ref, gw_ref, gb_ref,
    cot_ref, mask_ref, adj, run, feats, proj, gpre, rsend, crecv, rown,
    zs1, zr1, zs2, zr2, zxs, zxr, ys1, yr1, ys2, yr2, yxs, yxr,
    agg, gsum, ar_col, ar_row, gall, bias_own, bias_col, bias_row,
    send_sems, recv_sems, in_sems):
    row, col = lax.axis_index("row"), lax.axis_index("col")
    xh, y = row // 4, row % 4
    xl, z, core = col // 8, (col // 2) % 4, col % 2
    lines = Lines(send_sems, recv_sems)

    def dev(xh=xh, y=y, xl=xl, z=z, core=core):
        return (xh * 4 + y, (xl * 4 + z) * 2 + core)

    def at_y(step):
        return dev(y=(y + step) % 4)

    def at_z(step):
        return dev(z=(z + step) % 4)

    pair_x = dev(xh=1 - xh)
    near_x = dev(xl=1 - xl)
    other = dev(core=1 - core)
    col_mates, row_mates = [], []
    for flip in (1, 0):
        for step in (2, 1, 3, 0):
            for turn in (1, 0):
                if flip or step or turn:
                    to_xl, to_z, to_core = (xl + flip) % 2, (z + step) % 4, (core + turn) % 2
                    col_mates.append((dev(xl=to_xl, z=to_z, core=to_core), (to_xl * 4 + to_z) * 2 + to_core))
            if flip or step:
                to_xh, to_y = (xh + flip) % 2, (y + step) % 4
                row_mates.append((dev(xh=to_xh, y=to_y), to_xh * 4 + to_y))
    partners = [mate for mate, _ in row_mates + col_mates]
    cot_copy = pltpu.make_async_copy(cot_hbm, cot_ref, in_sems.at[0])
    mask_copy = pltpu.make_async_copy(mask_hbm, mask_ref, in_sems.at[1])
    adj_copy = pltpu.make_async_copy(adj_ref, adj, in_sems.at[2])
    for copy in (cot_copy, mask_copy, adj_copy):
        copy.start()

    barrier = pltpu.get_barrier_semaphore()
    for partner in partners:
        pl.semaphore_signal(barrier, inc=1, device_id=partner, device_id_type=MESH)

    gb_ref[...] = jnp.zeros_like(gb_ref)
    cot_copy.wait()
    mask_copy.wait()

    def project(b, _):
        nodes = pl.ds(pl.multiple_of(b * BLK, BLK), BLK)
        grad = cot_ref[nodes, :].astype(F32) * mask_ref[nodes, :].astype(F32)
        grad16 = grad.astype(BF16)
        gpre[nodes, :] = grad16
        gb_ref[...] += jnp.sum(grad16.astype(F32), axis=0, keepdims=True)
        turned = lax.dot_general(weight_ref[...], grad16, (((1,), (1,)), ((), ())), preferred_element_type=F32)
        proj[col * SHARD + b] = turned.astype(BF16)
        return 0

    lax.fori_loop(0, SHARD, project, 0, unroll=SHARD)
    pl.semaphore_wait(barrier, len(partners))

    def part(buf, shard, half):
        return buf.at[pl.ds(shard * SHARD + half * HALF, HALF)]

    class Gather:
        def __init__(self, buf, own, shard, pos, pair, ring, mate):
            self.buf, self.own, self.shard, self.pos, self.pair, self.ring, self.mate = buf, own, shard, pos, pair, ring, mate
            self.l0 = [lines.line() for _ in range(2)]
            self.l1 = [[lines.line() for _ in range(2)] for _ in range(2)]
            self.l2 = [lines.line() for _ in range(2)]
            self.l3 = [[lines.line() for _ in range(2)] for _ in range(2)]
            self.l4 = [lines.line() for _ in range(2)]

        def place(self, pair_step, step, half):
            pair = self.pair if pair_step == 0 else 1 - self.pair
            return part(self.buf, self.shard(pair, (self.pos + step) % 4), half)

        def begin(self):
            for half in range(2):
                for d in range(2):
                    h = half if d == 0 else 1 - half
                    lines.send(self.l1[d][h], self.own(h), self.place(0, 0, h), self.ring(1 - 2 * d))
                lines.send(self.l0[half], self.own(half), self.place(0, 0, half), self.mate)

        def got_mate(self, h):
            lines.wait(self.l0[h], self.place(1, 0, h), self.mate)
            return self.place(1, 0, h)

        def pass_mate(self, late, cross=True):
            for d in range(2):
                h = (1 - d if late else d) if cross else late
                lines.send(self.l3[d][h], self.place(1, 0, h), self.place(1, 0, h), self.ring(1 - 2 * d))

        def got_ring(self, kind, d, h):
            step = 2 * d - 1
            table = self.l1 if kind == 0 else self.l3
            place = self.place(kind, step, h)
            lines.wait(table[d][h], place, self.ring(step))
            return place

        def pass_ring(self, kind, d):
            step = 2 * d - 1
            table = self.l2 if kind == 0 else self.l4
            place = self.place(kind, step, d)
            lines.send(table[d], place, place, self.ring(-step))

        def got_far(self, kind, d):
            step = 2 * d - 1
            table = self.l2 if kind == 0 else self.l4
            place = self.place(kind, 2, d)
            lines.wait(table[d], place, self.ring(step))
            return place

    rows_g = Gather(feats, lambda h: feat_ref.at[pl.ds(h * HALF, HALF)],
                    lambda pair, pos: pair * 4 + pos, y, xh, at_y, pair_x)
    rows_g.begin()

    cols_g = Gather(proj, lambda h: part(proj, col, h),
                    lambda pair, pos: (pair * 4 + pos) * 2 + core, z, xl, at_z, near_x)
    cols_g.begin()

    across = []

    def cross(pair_step, step, h):
        line = lines.line()
        place = cols_g.place(pair_step, step, h)
        lines.send(line, place, place, other)
        pair = xl if pair_step == 0 else 1 - xl
        there = part(proj, (pair * 4 + (z + step) % 4) * 2 + 1 - core, h)
        across.append((line, there))

    feats[pl.ds(row * SHARD, SHARD)] = feat_ref[...]

    cross(0, 0, 0)
    cross(0, 0, 1)
    for d in range(2):
        rows_g.got_ring(0, d, d)
        rows_g.pass_ring(0, d)
    for d in range(2):
        cols_g.got_ring(0, d, d)
        cols_g.pass_ring(0, d)
    for h in range(2):
        rows_g.got_mate(h)
    for late in range(2):
        rows_g.pass_mate(late)
    for h in range(2):
        cols_g.got_mate(h)
        cols_g.pass_mate(h, False)
    for d in range(2):
        cross(0, 2 * d - 1, d)
        cross(1, 0, d)
    for d in range(2):
        cols_g.got_ring(0, d, 1 - d)
        cross(0, 2 * d - 1, 1 - d)
    for d in range(2):
        rows_g.got_ring(1, d, d)
        rows_g.pass_ring(1, d)
    for d in range(2):
        cols_g.got_far(0, d)
        cross(0, 2, d)
    for d in range(2):
        cols_g.got_ring(1, d, d)
        cols_g.pass_ring(1, d)
        cross(1, 2 * d - 1, d)
    for d in range(2):
        rows_g.got_ring(0, d, 1 - d)
        rows_g.got_far(0, d)
        rows_g.got_ring(1, d, 1 - d)
    for d in range(2):
        rows_g.got_far(1, d)
    adj_copy.wait()

    def spread(mates, source, target, place):
        used = [lines.line() for _ in mates]
        for line, (mate, theirs) in zip(used, mates):
            lines.send(line, source(theirs), target.at[place], mate)
        return used

    def collect(mates, used, target):
        for line, (mate, theirs) in zip(used, mates):
            lines.wait(line, target.at[theirs], mate)

    def added(ref):
        total = ref[0]
        for n in range(1, ref.shape[0]):
            total = total + ref[n]
        return total

    bias_own[...] = jnp.broadcast_to(gb_ref[...], bias_own.shape)
    bias_col[col] = bias_own[...]
    bias_lines = spread(col_mates, lambda theirs: bias_own, bias_col, col)

    slots = adj.shape[0]

    def forward(p, total):
        total = total * flt_ref[0, p] + jnp.dot(adj[idx_ref[0, p]], feats[idx_ref[1, p]], preferred_element_type=F32)
        run[p] = total
        return total

    lax.fori_loop(0, slots, forward, jnp.zeros((BLK, BLK), F32), unroll=64)

    def row_block(b):
        return run[idx_ref[2, b]] * flt_ref[1, b]

    order = [(pair_step, step) for pair_step in (1, 0) for step in (2, 1, -1, 0)]

    def spot(pair, pos, step):
        return pair * 4 + (pos + step) % 4

    core_lines = {}
    for pair_step, step in order:
        q = spot(1 - xl if pair_step else xl, z, step)

        def fill(b, _, q=q):
            rsend[q * SHARD + b] = row_block((q * 2 + 1 - core) * SHARD + b).astype(BF16)
            return 0

        lax.fori_loop(0, SHARD, fill, 0, unroll=SHARD)
        line = core_lines[pair_step, step] = lines.line()
        place = pl.ds(q * SHARD, SHARD)
        lines.send(line, rsend.at[place], crecv.at[place], other)

    def add_core(pair_step, step):
        q = spot(1 - xl if pair_step else xl, z, step)
        lines.wait(core_lines[pair_step, step], crecv.at[pl.ds(q * SHARD, SHARD)], other)

        def fill(b, _):
            rown[q * SHARD + b] = row_block((q * 2 + core) * SHARD + b) + crecv[q * SHARD + b].astype(F32)
            return 0

        lax.fori_loop(0, SHARD, fill, 0, unroll=SHARD)

    class Scatter:
        def __init__(self, s1, r1, s2, r2, xs, xr, term, ring, mate):
            self.s1, self.r1, self.s2, self.r2, self.xs, self.xr = s1, r1, s2, r2, xs, xr
            self.term, self.ring, self.mate = term, ring, mate
            self.l1 = [[lines.line() for _ in range(2)] for _ in range(2)]
            self.l2 = [[[lines.line() for _ in range(2)] for _ in range(2)] for _ in range(2)]
            self.lx = [lines.line() for _ in range(2)]

        def far(self, pair_step):
            for d in range(2):
                def fill(b, _, d=d):
                    b = d * HALF + b
                    self.s1[pair_step * SHARD + b] = self.term(pair_step, 2, b).astype(BF16)
                    return 0

                lax.fori_loop(0, HALF, fill, 0, unroll=HALF)
                place = pl.ds(pair_step * SHARD + d * HALF, HALF)
                lines.send(self.l1[pair_step][d], self.s1.at[place], self.r1.at[place], self.ring(1 - 2 * d))

        def near(self, pair_step, d, late):
            h = d if late else 1 - d
            base = (pair_step * 2 + d) * SHARD + h * HALF
            if late:
                place = pl.ds(pair_step * SHARD + d * HALF, HALF)
                lines.wait(self.l1[pair_step][d], self.r1.at[place], self.ring(2 * d - 1))

            def fill(b, _):
                value = self.term(pair_step, 1 - 2 * d, h * HALF + b)
                if late:
                    value = value + self.r1[pair_step * SHARD + d * HALF + b].astype(F32)
                self.s2[base + b] = value.astype(BF16)
                return 0

            lax.fori_loop(0, HALF, fill, 0, unroll=HALF)
            place = pl.ds(base, HALF)
            lines.send(self.l2[pair_step][d][h], self.s2.at[place], self.r2.at[place], self.ring(1 - 2 * d))

        def wait_near(self, pair_step, h):
            for d in range(2):
                place = pl.ds((pair_step * 2 + d) * SHARD + h * HALF, HALF)
                lines.wait(self.l2[pair_step][d][h], self.r2.at[place], self.ring(2 * d - 1))

        def total(self, pair_step, b):
            base = pair_step * 2 * SHARD + b
            return (self.term(pair_step, 0, b) + self.r2[base].astype(F32)) + self.r2[base + SHARD].astype(F32)

        def swap(self, h):
            self.wait_near(1, h)

            def fill(b, _):
                self.xs[h * HALF + b] = self.total(1, h * HALF + b).astype(BF16)
                return 0

            lax.fori_loop(0, HALF, fill, 0, unroll=HALF)
            place = pl.ds(h * HALF, HALF)
            lines.send(self.lx[h], self.xs.at[place], self.xr.at[place], self.mate)

        def finish(self, h, use):
            self.wait_near(0, h)
            lines.wait(self.lx[h], self.xr.at[pl.ds(h * HALF, HALF)], self.mate)

            def body(b, _):
                b = h * HALF + b
                use(b, self.total(0, b) + self.xr[b].astype(F32))
                return 0

            lax.fori_loop(0, HALF, body, 0, unroll=HALF)

    def row_term(pair_step, step, b):
        return rown[spot(1 - xl if pair_step else xl, z, step) * SHARD + b]

    rows_s = Scatter(zs1, zr1, zs2, zr2, zxs, zxr, row_term, at_z, near_x)
    for pair_step in (1, 0):
        add_core(pair_step, 2)
        rows_s.far(pair_step)
        for d in range(2):
            add_core(pair_step, 1 - 2 * d)
            rows_s.near(pair_step, d, False)
        add_core(pair_step, 0)
        if pair_step == 1:
            for d in range(2):
                cols_g.got_ring(1, d, 1 - d)
                cross(1, 2 * d - 1, 1 - d)
            for d in range(2):
                cols_g.got_far(1, d)
                cross(1, 2, d)
            for d in range(2):
                rows_s.near(1, d, True)

    for line, there in across:
        lines.wait(line, there, other)

    def backward(p, total):
        total = total * flt_ref[2, p] + jnp.dot(proj[idx_ref[4, p]], adj[idx_ref[3, p]], preferred_element_type=F32)
        run[p] = total
        return total

    lax.fori_loop(0, slots, backward, jnp.zeros((BLK, BLK), F32), unroll=32)

    collect(col_mates, bias_lines, bias_col)
    bias_row[row] = added(bias_col)
    bias_lines = spread(row_mates, lambda theirs: bias_row.at[row], bias_row, row)

    def col_term(pair_step, step, b):
        at = spot(1 - xh if pair_step else xh, y, step) * SHARD + b
        return run[idx_ref[5, at]] * flt_ref[3, at]

    cols_s = Scatter(ys1, yr1, ys2, yr2, yxs, yxr, col_term, at_y, pair_x)
    cols_s.far(1)
    for d in range(2):
        cols_s.near(1, d, False)
    for h in range(2):
        rows_s.swap(h)
    for d in range(2):
        rows_s.near(0, d, True)
    for d in range(2):
        cols_s.near(1, d, True)
    cols_s.far(0)
    for d in range(2):
        cols_s.near(0, d, False)
    def layer(b, value):
        nodes = pl.ds(pl.multiple_of(b * BLK, BLK), BLK)
        sums = value.astype(BF16)
        agg[b] = sums
        pre = jnp.dot(sums, weight_ref[...], preferred_element_type=F32) + bias_ref[...]
        out_ref[nodes, :] = (pre * mask_ref[nodes, :].astype(F32)).astype(BF16)

    for h in range(2):
        rows_s.finish(h, layer)

    def weight_term(b, total):
        nodes = pl.ds(pl.multiple_of(b * BLK, BLK), BLK)
        return total + lax.dot_general(agg[b], gpre[nodes, :], (((0,), (0,)), ((), ())), preferred_element_type=F32)

    gw_ref[...] = lax.fori_loop(0, SHARD, weight_term, jnp.zeros(gw_ref.shape, F32), unroll=SHARD)

    pieces, depth = gsum.shape[0], gsum.shape[1]
    for n in range(pieces):
        gsum[n] = gw_ref[pl.ds(n * depth, depth), :]
    used = spread(col_mates, lambda theirs: gsum.at[theirs], ar_col, col)
    ar_col[col] = gsum[col]
    for h in range(2):
        cols_s.swap(h)
    for d in range(2):
        cols_s.near(0, d, True)
    collect(col_mates, used, ar_col)
    ar_row[row] = added(ar_col)
    used = spread(row_mates, lambda theirs: ar_row.at[row], ar_row, row)
    collect(row_mates, used, ar_row)
    gall[col] = added(ar_row)
    used = spread(col_mates, lambda theirs: gall.at[col], gall, col)

    def store(b, value):
        gf_ref[b] = jnp.transpose(value).astype(BF16)

    for h in range(2):
        cols_s.finish(h, store)

    collect(row_mates, bias_lines, bias_row)
    gb_ref[...] = added(bias_row)[:1]
    collect(col_mates, used, gall)
    for n in range(pieces):
        gw_ref[pl.ds(n * depth, depth), :] = gall[n]
    lines.drain()
    assert lines.used <= N_LINES


def local(features, weight, bias, adjacency, block_rows, block_cols, block_count, cotangent, relu_mask):
    slots = adjacency.shape[2]
    vmem, smem, hbm = (pl.BlockSpec(memory_space=m) for m in (pltpu.VMEM, pltpu.SMEM, pl.ANY))
    idx, flt = pl.pallas_call(
        plan_kernel,
        out_shape=(jax.ShapeDtypeStruct((8, slots), jnp.int32), jax.ShapeDtypeStruct((8, slots), F32)),
        in_specs=[smem, vmem, vmem],
        out_specs=(vmem, vmem),
        name="plan",
    )(block_count, block_rows[0], block_cols[0])
    hid = weight.shape[1]

    def blocks(n, dtype=BF16):
        return pltpu.VMEM((n, BLK, BLK), dtype)

    scratch = [
        pltpu.VMEM((1024, hid), BF16), pltpu.VMEM((1024, hid), jnp.int32),
        blocks(slots), blocks(slots, F32), blocks(64), blocks(128), pltpu.VMEM((1024, hid), BF16),
        blocks(64), blocks(64), blocks(64, F32)]
    for _ in range(2):
        scratch += [blocks(16), blocks(16), blocks(32), blocks(32), blocks(8), blocks(8)]
    piece = (8, hid)
    scratch += [blocks(8)] + [pltpu.VMEM((n,) + piece, F32) for n in (16, 16, 8, 16)]
    scratch += [pltpu.VMEM(piece, F32)] + [pltpu.VMEM((n,) + piece, F32) for n in (16, 8)]
    scratch += [pltpu.SemaphoreType.DMA((N_LINES,)), pltpu.SemaphoreType.DMA((N_LINES,)), pltpu.SemaphoreType.DMA((3,))]
    out, gf, gw, gb = pl.pallas_call(
        layer_kernel,
        out_shape=(
            jax.ShapeDtypeStruct((1024, hid), BF16),
            jax.ShapeDtypeStruct((SHARD, BLK, BLK), BF16),
            jax.ShapeDtypeStruct(weight.shape, F32),
            jax.ShapeDtypeStruct((1, hid), F32),
        ),
        in_specs=[smem, smem, vmem, vmem, vmem, hbm, hbm, hbm],
        out_specs=(vmem, vmem, vmem, vmem),
        scratch_shapes=scratch,
        compiler_params=pltpu.CompilerParams(collective_id=0, has_side_effects=True, vmem_limit_bytes=60 * 2**20),
        name="layer",
    )(idx, flt, features.reshape(SHARD, BLK, BLK), weight, bias.reshape(1, hid), cotangent, relu_mask,
      adjacency.reshape(slots, BLK, BLK))
    results = (out, gf, gw, gb)
    out, gf, gw, gb = pl.pallas_call(
        hand_on_kernel,
        out_shape=tuple(jax.ShapeDtypeStruct(r.shape, r.dtype) for r in results),
        in_specs=[vmem] * 4,
        out_specs=(vmem,) * 4,
        name="hand_on",
    )(*results)
    return out, gf.reshape(1024, BLK), gw, gb.reshape(hid)


def solution(mesh):
    in_specs = (
        P(("col", "row"), None),
        P(),
        P(),
        P("row", "col", None, None, None),
        P("row", "col", None),
        P("row", "col", None),
        P("row", "col"),
        P(("row", "col"), None),
        P(("row", "col"), None),
    )
    out_specs = (P(("row", "col"), None), P(("col", "row"), None), P(), P())
    return jax.shard_map(local, mesh=mesh, in_specs=in_specs, out_specs=out_specs, check_vma=False)
```

```python
import functools

import jax
import jax.numpy as jnp
from jax import lax
from jax.experimental import pallas as pl
from jax.experimental.pallas import tpu as pltpu
from jax.sharding import PartitionSpec as P

F32 = jnp.float32
BF16 = jnp.bfloat16
MESH = pl.DeviceIdType.MESH
BLK = 128
SHARD = 8
HALF = 4


def plan(count_ref, rows_ref, cols_ref, idx_ref, flt_ref):
    n = rows_ref.shape[1]
    count = count_ref[0, 0]
    lane = lax.broadcasted_iota(jnp.int32, (n, n), 1)
    sub = lax.broadcasted_iota(jnp.int32, (n, n), 0)
    one, zero = jnp.ones((n, n), jnp.int32), jnp.zeros((n, n), jnp.int32)
    eye = lane == sub
    live_l, live_c = lane < count, sub < count
    row_l = jnp.broadcast_to(rows_ref[...], (n, n))
    col_l = jnp.broadcast_to(cols_ref[...], (n, n))
    row_c = jnp.broadcast_to(jnp.sum(jnp.where(eye, row_l, zero), axis=1, keepdims=True), (n, n))
    col_c = jnp.broadcast_to(jnp.sum(jnp.where(eye, col_l, zero), axis=1, keepdims=True), (n, n))
    idx_ref[...] = jnp.zeros_like(idx_ref)
    flt_ref[...] = jnp.zeros_like(flt_ref)
    tops = (127, 63)
    for side, (major_l, major_c, minor_c) in enumerate(((row_l, row_c, col_c), (col_l, col_c, row_c))):
        far = jnp.full((n, n), 65536, jnp.int32)
        key_l = jnp.where(live_l, major_l * n, far) + lane
        key_c = jnp.where(live_c, major_c * n, far) + sub
        rank = jnp.sum(jnp.where(key_l < key_c, one, zero), axis=1, keepdims=True)
        hot = jnp.broadcast_to(rank, (n, n)) == lane
        same = jnp.where((major_l == major_c) & (lane < sub) & live_l, one, zero)
        keep = jnp.broadcast_to(jnp.minimum(jnp.sum(same, axis=1, keepdims=True), 1), (n, n))
        slot = jnp.sum(jnp.where(hot, sub, zero), axis=0, keepdims=True)
        minor = jnp.sum(jnp.where(hot, minor_c, zero), axis=0, keepdims=True)
        keep_sorted = jnp.sum(jnp.where(hot, keep, zero), axis=0, keepdims=True)
        upto = jnp.sum(jnp.where((major_c <= lane) & live_c, one, zero), axis=0, keepdims=True)
        here = jnp.sum(jnp.where((major_c == lane) & live_c, one, zero), axis=0, keepdims=True)
        idx_ref[3 * side : 3 * side + 1, :] = jnp.clip(slot, 0, n - 1)
        idx_ref[3 * side + 1 : 3 * side + 2, :] = jnp.clip(minor, 0, tops[1 - side])
        idx_ref[3 * side + 2 : 3 * side + 3, :] = jnp.clip(upto - 1, 0, n - 1)
        flt_ref[2 * side : 2 * side + 1, :] = keep_sorted.astype(F32)
        flt_ref[2 * side + 1 : 2 * side + 2, :] = jnp.minimum(here, 1).astype(F32)


def hand_on_kernel(*refs):
    half = len(refs) // 2
    for source, target in zip(refs[:half], refs[half:]):
        target[...] = source[...]


class Lines:
    def __init__(self, send_sems, recv_sems):
        self.send_sems, self.recv_sems, self.used, self.sent = send_sems, recv_sems, 0, []

    def line(self):
        self.used += 1
        return self.used - 1

    def send(self, line, src, dst, device):
        copy = pltpu.make_async_remote_copy(
            src_ref=src, dst_ref=dst, send_sem=self.send_sems.at[line], recv_sem=self.recv_sems.at[line],
            device_id=device, device_id_type=MESH)
        copy.start()
        self.sent.append(copy)

    def wait(self, line, dst, device):
        pltpu.make_async_remote_copy(
            src_ref=dst, dst_ref=dst, send_sem=self.send_sems.at[line], recv_sem=self.recv_sems.at[line],
            device_id=device, device_id_type=MESH).wait_recv()

    def drain(self):
        for copy in self.sent:
            copy.wait_send()


N_LINES = 160


def layer_kernel(
    count_ref, rows_ref, cols_ref, feat_ref, weight_ref, bias_ref, cot_hbm, mask_hbm, adj_ref,
    out_ref, gf_ref, gw_ref, gb_ref,
    idx_vmem, flt_vmem, idx_ref, flt_ref, cot_ref, mask_ref, adj, run, feats, proj, gpre, rsend, crecv, rown,
    zs1, zr1, zs2, zr2, zxs, zxr, ys1, yr1, ys2, yr2, yxs, yxr,
    agg, gsum, ar_col, ar_row, gall, bias_own, bias_col, bias_row,
    send_sems, recv_sems, in_sems):
    row, col = lax.axis_index("row"), lax.axis_index("col")
    xh, y = row // 4, row % 4
    xl, z, core = col // 8, (col // 2) % 4, col % 2
    lines = Lines(send_sems, recv_sems)

    def dev(xh=xh, y=y, xl=xl, z=z, core=core):
        return (xh * 4 + y, (xl * 4 + z) * 2 + core)

    def at_y(step):
        return dev(y=(y + step) % 4)

    def at_z(step):
        return dev(z=(z + step) % 4)

    pair_x = dev(xh=1 - xh)
    near_x = dev(xl=1 - xl)
    other = dev(core=1 - core)
    col_mates, row_mates = [], []
    for flip in (1, 0):
        for step in (2, 1, 3, 0):
            for turn in (1, 0):
                if flip or step or turn:
                    to_xl, to_z, to_core = (xl + flip) % 2, (z + step) % 4, (core + turn) % 2
                    col_mates.append((dev(xl=to_xl, z=to_z, core=to_core), (to_xl * 4 + to_z) * 2 + to_core))
            if flip or step:
                to_xh, to_y = (xh + flip) % 2, (y + step) % 4
                row_mates.append((dev(xh=to_xh, y=to_y), to_xh * 4 + to_y))
    partners = [mate for mate, _ in row_mates + col_mates]
    cot_copy = pltpu.make_async_copy(cot_hbm, cot_ref, in_sems.at[0])
    mask_copy = pltpu.make_async_copy(mask_hbm, mask_ref, in_sems.at[1])
    adj_copy = pltpu.make_async_copy(adj_ref, adj, in_sems.at[2])
    for copy in (cot_copy, mask_copy, adj_copy):
        copy.start()

    barrier = pltpu.get_barrier_semaphore()
    for partner in partners:
        pl.semaphore_signal(barrier, inc=1, device_id=partner, device_id_type=MESH)

    gb_ref[...] = jnp.zeros_like(gb_ref)
    cot_copy.wait()
    mask_copy.wait()

    def project(b, _):
        nodes = pl.ds(pl.multiple_of(b * BLK, BLK), BLK)
        grad = cot_ref[nodes, :].astype(F32) * mask_ref[nodes, :].astype(F32)
        grad16 = grad.astype(BF16)
        gpre[nodes, :] = grad16
        gb_ref[...] += jnp.sum(grad16.astype(F32), axis=0, keepdims=True)
        turned = lax.dot_general(weight_ref[...], grad16, (((1,), (1,)), ((), ())), preferred_element_type=F32)
        proj[col * SHARD + b] = turned.astype(BF16)
        return 0

    lax.fori_loop(0, SHARD, project, 0, unroll=SHARD)
    pl.semaphore_wait(barrier, len(partners))

    def part(buf, shard, half):
        return buf.at[pl.ds(shard * SHARD + half * HALF, HALF)]

    class Gather:
        def __init__(self, buf, own, shard, pos, pair, ring, mate):
            self.buf, self.own, self.shard, self.pos, self.pair, self.ring, self.mate = buf, own, shard, pos, pair, ring, mate
            self.l0 = [lines.line() for _ in range(2)]
            self.l1 = [[lines.line() for _ in range(2)] for _ in range(2)]
            self.l2 = [lines.line() for _ in range(2)]
            self.l3 = [[lines.line() for _ in range(2)] for _ in range(2)]
            self.l4 = [lines.line() for _ in range(2)]

        def place(self, pair_step, step, half):
            pair = self.pair if pair_step == 0 else 1 - self.pair
            return part(self.buf, self.shard(pair, (self.pos + step) % 4), half)

        def begin(self):
            for half in range(2):
                for d in range(2):
                    h = half if d == 0 else 1 - half
                    lines.send(self.l1[d][h], self.own(h), self.place(0, 0, h), self.ring(1 - 2 * d))
                lines.send(self.l0[half], self.own(half), self.place(0, 0, half), self.mate)

        def got_mate(self, h):
            lines.wait(self.l0[h], self.place(1, 0, h), self.mate)
            return self.place(1, 0, h)

        def pass_mate(self, late, cross=True):
            for d in range(2):
                h = (1 - d if late else d) if cross else late
                lines.send(self.l3[d][h], self.place(1, 0, h), self.place(1, 0, h), self.ring(1 - 2 * d))

        def got_ring(self, kind, d, h):
            step = 2 * d - 1
            table = self.l1 if kind == 0 else self.l3
            place = self.place(kind, step, h)
            lines.wait(table[d][h], place, self.ring(step))
            return place

        def pass_ring(self, kind, d):
            step = 2 * d - 1
            table = self.l2 if kind == 0 else self.l4
            place = self.place(kind, step, d)
            lines.send(table[d], place, place, self.ring(-step))

        def got_far(self, kind, d):
            step = 2 * d - 1
            table = self.l2 if kind == 0 else self.l4
            place = self.place(kind, 2, d)
            lines.wait(table[d], place, self.ring(step))
            return place

    rows_g = Gather(feats, lambda h: feat_ref.at[pl.ds(h * HALF, HALF)],
                    lambda pair, pos: pair * 4 + pos, y, xh, at_y, pair_x)
    rows_g.begin()

    cols_g = Gather(proj, lambda h: part(proj, col, h),
                    lambda pair, pos: (pair * 4 + pos) * 2 + core, z, xl, at_z, near_x)
    cols_g.begin()

    across = []

    def cross(pair_step, step, h):
        line = lines.line()
        place = cols_g.place(pair_step, step, h)
        lines.send(line, place, place, other)
        pair = xl if pair_step == 0 else 1 - xl
        there = part(proj, (pair * 4 + (z + step) % 4) * 2 + 1 - core, h)
        across.append((line, there))

    feats[pl.ds(row * SHARD, SHARD)] = feat_ref[...]

    cross(0, 0, 0)
    cross(0, 0, 1)
    plan(count_ref, rows_ref, cols_ref, idx_vmem, flt_vmem)
    idx_copy = pltpu.make_async_copy(idx_vmem, idx_ref, in_sems.at[3])
    flt_copy = pltpu.make_async_copy(flt_vmem, flt_ref, in_sems.at[4])
    idx_copy.start()
    flt_copy.start()
    for d in range(2):
        rows_g.got_ring(0, d, d)
        rows_g.pass_ring(0, d)
    for d in range(2):
        cols_g.got_ring(0, d, d)
        cols_g.pass_ring(0, d)
    for h in range(2):
        rows_g.got_mate(h)
    for late in range(2):
        rows_g.pass_mate(late)
    for h in range(2):
        cols_g.got_mate(h)
        cols_g.pass_mate(h, False)
    for d in range(2):
        cross(0, 2 * d - 1, d)
        cross(1, 0, d)
    for d in range(2):
        cols_g.got_ring(0, d, 1 - d)
        cross(0, 2 * d - 1, 1 - d)
    for d in range(2):
        rows_g.got_ring(1, d, d)
        rows_g.pass_ring(1, d)
    for d in range(2):
        cols_g.got_far(0, d)
        cross(0, 2, d)
    for d in range(2):
        cols_g.got_ring(1, d, d)
        cols_g.pass_ring(1, d)
        cross(1, 2 * d - 1, d)
    for d in range(2):
        rows_g.got_ring(0, d, 1 - d)
        rows_g.got_far(0, d)
        rows_g.got_ring(1, d, 1 - d)
    for d in range(2):
        rows_g.got_far(1, d)
    adj_copy.wait()
    idx_copy.wait()
    flt_copy.wait()

    def spread(mates, source, target, place):
        used = [lines.line() for _ in mates]
        for line, (mate, theirs) in zip(used, mates):
            lines.send(line, source(theirs), target.at[place], mate)
        return used

    def collect(mates, used, target):
        for line, (mate, theirs) in zip(used, mates):
            lines.wait(line, target.at[theirs], mate)

    def added(ref):
        total = ref[0]
        for n in range(1, ref.shape[0]):
            total = total + ref[n]
        return total

    bias_own[0] = gb_ref[...]
    bias_col[col] = gb_ref[...]
    bias_lines = spread(col_mates, lambda theirs: bias_own.at[0], bias_col, col)

    slots = adj.shape[0]

    def forward(p, total):
        total = total * flt_ref[0, p] + jnp.dot(adj[idx_ref[0, p]], feats[idx_ref[1, p]], preferred_element_type=F32)
        run[p] = total
        return total

    lax.fori_loop(0, slots, forward, jnp.zeros((BLK, BLK), F32), unroll=64)

    def row_block(b):
        return run[idx_ref[2, b]] * flt_ref[1, b]

    order = [(1, 2), (1, 1), (1, -1), (0, 1), (0, -1), (0, 2), (1, 0), (0, 0)]

    def spot(pair, pos, step):
        return pair * 4 + (pos + step) % 4

    core_lines = {}
    for pair_step, step in order:
        q = spot(1 - xl if pair_step else xl, z, step)

        def fill(b, _, q=q):
            rsend[q * SHARD + b] = row_block((q * 2 + 1 - core) * SHARD + b).astype(BF16)
            return 0

        lax.fori_loop(0, SHARD, fill, 0, unroll=SHARD)
        line = core_lines[pair_step, step] = lines.line()
        place = pl.ds(q * SHARD, SHARD)
        lines.send(line, rsend.at[place], crecv.at[place], other)

    def add_core(pair_step, step):
        q = spot(1 - xl if pair_step else xl, z, step)
        lines.wait(core_lines[pair_step, step], crecv.at[pl.ds(q * SHARD, SHARD)], other)

        def fill(b, _):
            rown[q * SHARD + b] = row_block((q * 2 + core) * SHARD + b) + crecv[q * SHARD + b].astype(F32)
            return 0

        lax.fori_loop(0, SHARD, fill, 0, unroll=SHARD)

    class Scatter:
        def __init__(self, s1, r1, s2, r2, xs, xr, term, ring, mate, far_by_mate):
            self.s1, self.r1, self.s2, self.r2, self.xs, self.xr = s1, r1, s2, r2, xs, xr
            self.term, self.ring, self.mate, self.far_by_mate = term, ring, mate, far_by_mate
            self.l1 = [[lines.line() for _ in range(2)] for _ in range(2)]
            self.l2 = [[[lines.line() for _ in range(2)] for _ in range(2)] for _ in range(2)]
            self.lx = [lines.line() for _ in range(2)]

        def far(self, pair_step):
            for d in range(2):
                if self.far_by_mate and pair_step == 0:
                    lines.wait(self.l1[1][d], self.r1.at[pl.ds(SHARD + d * HALF, HALF)], self.mate)

                def fill(b, _, d=d):
                    b = d * HALF + b
                    value = self.term(pair_step, 2, b)
                    if self.far_by_mate and pair_step == 0:
                        value = value + self.r1[SHARD + b].astype(F32)
                    self.s1[pair_step * SHARD + b] = value.astype(BF16)
                    return 0

                lax.fori_loop(0, HALF, fill, 0, unroll=HALF)
                place = pl.ds(pair_step * SHARD + d * HALF, HALF)
                lines.send(self.l1[pair_step][d], self.s1.at[place], self.r1.at[place],
                           self.mate if self.far_by_mate and pair_step else self.ring(1 - 2 * d))

        def near(self, pair_step, d, late):
            h = d if late else 1 - d
            base = (pair_step * 2 + d) * SHARD + h * HALF
            passing = late and not (self.far_by_mate and pair_step)
            if passing:
                place = pl.ds(pair_step * SHARD + d * HALF, HALF)
                lines.wait(self.l1[pair_step][d], self.r1.at[place], self.ring(2 * d - 1))

            def fill(b, _):
                value = self.term(pair_step, 1 - 2 * d, h * HALF + b)
                if passing:
                    value = value + self.r1[pair_step * SHARD + d * HALF + b].astype(F32)
                self.s2[base + b] = value.astype(BF16)
                return 0

            lax.fori_loop(0, HALF, fill, 0, unroll=HALF)
            place = pl.ds(base, HALF)
            lines.send(self.l2[pair_step][d][h], self.s2.at[place], self.r2.at[place], self.ring(1 - 2 * d))

        def wait_near(self, pair_step, h):
            for d in range(2):
                place = pl.ds((pair_step * 2 + d) * SHARD + h * HALF, HALF)
                lines.wait(self.l2[pair_step][d][h], self.r2.at[place], self.ring(2 * d - 1))

        def total(self, pair_step, b):
            base = pair_step * 2 * SHARD + b
            return (self.term(pair_step, 0, b) + self.r2[base].astype(F32)) + self.r2[base + SHARD].astype(F32)

        def swap(self, h):
            self.wait_near(1, h)

            def fill(b, _):
                self.xs[h * HALF + b] = self.total(1, h * HALF + b).astype(BF16)
                return 0

            lax.fori_loop(0, HALF, fill, 0, unroll=HALF)
            place = pl.ds(h * HALF, HALF)
            lines.send(self.lx[h], self.xs.at[place], self.xr.at[place], self.mate)

        def finish(self, h, use):
            self.wait_near(0, h)
            lines.wait(self.lx[h], self.xr.at[pl.ds(h * HALF, HALF)], self.mate)

            def body(b, _):
                b = h * HALF + b
                use(b, self.total(0, b) + self.xr[b].astype(F32))
                return 0

            lax.fori_loop(0, HALF, body, 0, unroll=HALF)

    def row_term(pair_step, step, b):
        return rown[spot(1 - xl if pair_step else xl, z, step) * SHARD + b]

    rows_s = Scatter(zs1, zr1, zs2, zr2, zxs, zxr, row_term, at_z, near_x, True)
    add_core(1, 2)
    rows_s.far(1)
    for d in range(2):
        add_core(1, 1 - 2 * d)
        rows_s.near(1, d, False)
    for d in range(2):
        rows_s.near(1, d, True)
    for d in range(2):
        add_core(0, 1 - 2 * d)
        rows_s.near(0, d, False)
    add_core(0, 2)
    for pair_step in (1, 0):
        add_core(pair_step, 0)
    for d in range(2):
        cols_g.got_ring(1, d, 1 - d)
        cross(1, 2 * d - 1, 1 - d)
    for d in range(2):
        cols_g.got_far(1, d)
        cross(1, 2, d)

    for line, there in across:
        lines.wait(line, there, other)

    def backward(p, total):
        total = total * flt_ref[2, p] + jnp.dot(proj[idx_ref[4, p]], adj[idx_ref[3, p]], preferred_element_type=F32)
        run[p] = total
        return total

    lax.fori_loop(0, slots, backward, jnp.zeros((BLK, BLK), F32), unroll=32)

    def col_term(pair_step, step, b):
        at = spot(1 - xh if pair_step else xh, y, step) * SHARD + b
        return run[idx_ref[5, at]] * flt_ref[3, at]

    cols_s = Scatter(ys1, yr1, ys2, yr2, yxs, yxr, col_term, at_y, pair_x, False)
    cols_s.far(1)
    for d in range(2):
        cols_s.near(1, d, False)
    rows_s.far(0)
    for h in range(2):
        rows_s.swap(h)
    for d in range(2):
        cols_s.near(1, d, True)
    cols_s.far(0)
    for d in range(2):
        cols_s.near(0, d, False)
    for d in range(2):
        rows_s.near(0, d, True)

    collect(col_mates, bias_lines, bias_col)
    bias_row[row] = added(bias_col)
    bias_lines = spread(row_mates, lambda theirs: bias_row.at[row], bias_row, row)

    def aggregate(b, value):
        agg[b] = value.astype(BF16)

    def layer(b, _):
        nodes = pl.ds(pl.multiple_of(b * BLK, BLK), BLK)
        pre = jnp.dot(agg[b], weight_ref[...], preferred_element_type=F32) + bias_ref[...]
        out_ref[nodes, :] = (pre * mask_ref[nodes, :].astype(F32)).astype(BF16)
        return 0

    for h in range(2):
        rows_s.finish(h, aggregate)

    def weight_term(b, total):
        nodes = pl.ds(pl.multiple_of(b * BLK, BLK), BLK)
        return total + lax.dot_general(agg[b], gpre[nodes, :], (((0,), (0,)), ((), ())), preferred_element_type=F32)

    gw_ref[...] = lax.fori_loop(0, SHARD, weight_term, jnp.zeros(gw_ref.shape, F32), unroll=SHARD)

    pieces, depth = gsum.shape[0], gsum.shape[1]
    for n in range(pieces):
        gsum[n] = gw_ref[pl.ds(n * depth, depth), :]
    used = spread(col_mates, lambda theirs: gsum.at[theirs], ar_col, col)
    ar_col[col] = gsum[col]
    lax.fori_loop(0, SHARD, layer, 0, unroll=SHARD)
    for h in range(2):
        cols_s.swap(h)
    for d in range(2):
        cols_s.near(0, d, True)
    collect(col_mates, used, ar_col)
    ar_row[row] = added(ar_col)
    used = spread(row_mates, lambda theirs: ar_row.at[row], ar_row, row)
    collect(row_mates, used, ar_row)
    gall[col] = added(ar_row)
    used = spread(col_mates, lambda theirs: gall.at[col], gall, col)

    def store(b, value):
        gf_ref[b] = jnp.transpose(value).astype(BF16)

    for h in range(2):
        cols_s.finish(h, store)

    collect(row_mates, bias_lines, bias_row)
    gb_ref[...] = added(bias_row)
    collect(col_mates, used, gall)
    for n in range(pieces):
        gw_ref[pl.ds(n * depth, depth), :] = gall[n]
    lines.drain()
    assert lines.used <= N_LINES


def local(features, weight, bias, adjacency, block_rows, block_cols, block_count, cotangent, relu_mask):
    slots = adjacency.shape[2]
    vmem, smem, hbm = (pl.BlockSpec(memory_space=m) for m in (pltpu.VMEM, pltpu.SMEM, pl.ANY))
    hid = weight.shape[1]

    def blocks(n, dtype=BF16):
        return pltpu.VMEM((n, BLK, BLK), dtype)

    plan_shape = (8, slots)
    scratch = [
        pltpu.VMEM(plan_shape, jnp.int32), pltpu.VMEM(plan_shape, F32), pltpu.SMEM(plan_shape, jnp.int32), pltpu.SMEM(plan_shape, F32),
        pltpu.VMEM((1024, hid), BF16), pltpu.VMEM((1024, hid), jnp.int32),
        blocks(slots), blocks(slots, F32), blocks(64), blocks(128), pltpu.VMEM((1024, hid), BF16),
        blocks(64), blocks(64), blocks(64, F32)]
    for _ in range(2):
        scratch += [blocks(16), blocks(16), blocks(32), blocks(32), blocks(8), blocks(8)]
    piece = (8, hid)
    scratch += [blocks(8)] + [pltpu.VMEM((n,) + piece, F32) for n in (16, 16, 8, 16)]
    scratch += [pltpu.VMEM((n, 1, hid), F32) for n in (1, 16, 8)]
    scratch += [pltpu.SemaphoreType.DMA((N_LINES,)), pltpu.SemaphoreType.DMA((N_LINES,)), pltpu.SemaphoreType.DMA((5,))]
    out, gf, gw, gb = pl.pallas_call(
        layer_kernel,
        out_shape=(
            jax.ShapeDtypeStruct((1024, hid), BF16),
            jax.ShapeDtypeStruct((SHARD, BLK, BLK), BF16),
            jax.ShapeDtypeStruct(weight.shape, F32),
            jax.ShapeDtypeStruct((1, hid), F32),
        ),
        in_specs=[smem, vmem, vmem, vmem, vmem, vmem, hbm, hbm, hbm],
        out_specs=(vmem, vmem, vmem, vmem),
        scratch_shapes=scratch,
        compiler_params=pltpu.CompilerParams(collective_id=0, has_side_effects=True, vmem_limit_bytes=60 * 2**20),
        name="layer",
    )(block_count, block_rows[0], block_cols[0], features.reshape(SHARD, BLK, BLK), weight, bias.reshape(1, hid), cotangent, relu_mask,
      adjacency.reshape(slots, BLK, BLK))
    results = (out, gf, gw, gb)
    out, gf, gw, gb = pl.pallas_call(
        hand_on_kernel,
        out_shape=tuple(jax.ShapeDtypeStruct(r.shape, r.dtype) for r in results),
        in_specs=[vmem] * 4,
        out_specs=(vmem,) * 4,
        name="hand_on",
    )(*results)
    return out, gf.reshape(1024, BLK), gw, gb.reshape(hid)


def solution(mesh):
    in_specs = (
        P(("col", "row"), None),
        P(),
        P(),
        P("row", "col", None, None, None),
        P("row", "col", None),
        P("row", "col", None),
        P("row", "col"),
        P(("row", "col"), None),
        P(("row", "col"), None),
    )
    out_specs = (P(("row", "col"), None), P(("col", "row"), None), P(), P())
    return jax.shard_map(local, mesh=mesh, in_specs=in_specs, out_specs=out_specs, check_vma=False)
```

```python
import functools

import jax
import jax.numpy as jnp
from jax import lax
from jax.experimental import pallas as pl
from jax.experimental.pallas import tpu as pltpu
from jax.sharding import PartitionSpec as P

F32 = jnp.float32
BF16 = jnp.bfloat16
MESH = pl.DeviceIdType.MESH
BLK = 128
SHARD = 8
HALF = 4


def plan(count_ref, rows_ref, cols_ref, idx_ref, flt_ref):
    n = rows_ref.shape[1]
    count = count_ref[0, 0]
    lane = lax.broadcasted_iota(jnp.int32, (n, n), 1)
    sub = lax.broadcasted_iota(jnp.int32, (n, n), 0)
    one, zero = jnp.ones((n, n), jnp.int32), jnp.zeros((n, n), jnp.int32)
    eye = lane == sub
    live_l, live_c = lane < count, sub < count
    row_l = jnp.broadcast_to(rows_ref[...], (n, n))
    col_l = jnp.broadcast_to(cols_ref[...], (n, n))
    row_c = jnp.broadcast_to(jnp.sum(jnp.where(eye, row_l, zero), axis=1, keepdims=True), (n, n))
    col_c = jnp.broadcast_to(jnp.sum(jnp.where(eye, col_l, zero), axis=1, keepdims=True), (n, n))
    idx_ref[...] = jnp.zeros_like(idx_ref)
    flt_ref[...] = jnp.zeros_like(flt_ref)
    tops = (127, 63)
    for side, (major_l, major_c, minor_c) in enumerate(((row_l, row_c, col_c), (col_l, col_c, row_c))):
        far = jnp.full((n, n), 65536, jnp.int32)
        key_l = jnp.where(live_l, major_l * n, far) + lane
        key_c = jnp.where(live_c, major_c * n, far) + sub
        rank = jnp.sum(jnp.where(key_l < key_c, one, zero), axis=1, keepdims=True)
        hot = jnp.broadcast_to(rank, (n, n)) == lane
        same = jnp.where((major_l == major_c) & (lane < sub) & live_l, one, zero)
        keep = jnp.broadcast_to(jnp.minimum(jnp.sum(same, axis=1, keepdims=True), 1), (n, n))
        slot = jnp.sum(jnp.where(hot, sub, zero), axis=0, keepdims=True)
        minor = jnp.sum(jnp.where(hot, minor_c, zero), axis=0, keepdims=True)
        keep_sorted = jnp.sum(jnp.where(hot, keep, zero), axis=0, keepdims=True)
        upto = jnp.sum(jnp.where((major_c <= lane) & live_c, one, zero), axis=0, keepdims=True)
        here = jnp.sum(jnp.where((major_c == lane) & live_c, one, zero), axis=0, keepdims=True)
        idx_ref[3 * side : 3 * side + 1, :] = jnp.clip(slot, 0, n - 1)
        idx_ref[3 * side + 1 : 3 * side + 2, :] = jnp.clip(minor, 0, tops[1 - side])
        idx_ref[3 * side + 2 : 3 * side + 3, :] = jnp.clip(upto - 1, 0, n - 1)
        flt_ref[2 * side : 2 * side + 1, :] = keep_sorted.astype(F32)
        flt_ref[2 * side + 1 : 2 * side + 2, :] = jnp.minimum(here, 1).astype(F32)


def hand_on_kernel(*refs):
    half = len(refs) // 2
    for source, target in zip(refs[:half], refs[half:]):
        target[...] = source[...]


class Lines:
    def __init__(self, send_sems, recv_sems):
        self.send_sems, self.recv_sems, self.used, self.sent = send_sems, recv_sems, 0, []

    def line(self):
        self.used += 1
        return self.used - 1

    def send(self, line, src, dst, device):
        copy = pltpu.make_async_remote_copy(
            src_ref=src, dst_ref=dst, send_sem=self.send_sems.at[line], recv_sem=self.recv_sems.at[line],
            device_id=device, device_id_type=MESH)
        copy.start()
        self.sent.append(copy)

    def wait(self, line, dst, device):
        pltpu.make_async_remote_copy(
            src_ref=dst, dst_ref=dst, send_sem=self.send_sems.at[line], recv_sem=self.recv_sems.at[line],
            device_id=device, device_id_type=MESH).wait_recv()

    def drain(self):
        for copy in self.sent:
            copy.wait_send()


N_LINES = 160


def layer_kernel(
    count_ref, rows_ref, cols_ref, feat_ref, weight_ref, bias_ref, cot_hbm, mask_hbm, adj_ref,
    out_ref, gf_ref, gw_ref, gb_ref,
    idx_vmem, flt_vmem, idx_ref, flt_ref, cot_ref, mask_ref, adj, run, feats, proj, gpre, rsend, crecv, rown,
    zs1, zr1, zs2, zr2, zxs, zxr, ys1, yr1, ys2, yr2, yxs, yxr,
    agg, gsum, ar_col, ar_row, gall, bias_own, bias_col, bias_row,
    send_sems, recv_sems, in_sems):
    row, col = lax.axis_index("row"), lax.axis_index("col")
    xh, y = row // 4, row % 4
    xl, z, core = col // 8, (col // 2) % 4, col % 2
    lines = Lines(send_sems, recv_sems)

    def dev(xh=xh, y=y, xl=xl, z=z, core=core):
        return (xh * 4 + y, (xl * 4 + z) * 2 + core)

    def at_y(step):
        return dev(y=(y + step) % 4)

    def at_z(step):
        return dev(z=(z + step) % 4)

    pair_x = dev(xh=1 - xh)
    near_x = dev(xl=1 - xl)
    other = dev(core=1 - core)
    col_mates, row_mates = [], []
    for flip in (1, 0):
        for step in (2, 1, 3, 0):
            for turn in (1, 0):
                if flip or step or turn:
                    to_xl, to_z, to_core = (xl + flip) % 2, (z + step) % 4, (core + turn) % 2
                    col_mates.append((dev(xl=to_xl, z=to_z, core=to_core), (to_xl * 4 + to_z) * 2 + to_core))
            if flip or step:
                to_xh, to_y = (xh + flip) % 2, (y + step) % 4
                row_mates.append((dev(xh=to_xh, y=to_y), to_xh * 4 + to_y))
    partners = [mate for mate, _ in row_mates + col_mates]
    cot_copy = pltpu.make_async_copy(cot_hbm, cot_ref, in_sems.at[0])
    mask_copy = pltpu.make_async_copy(mask_hbm, mask_ref, in_sems.at[1])
    adj_copy = pltpu.make_async_copy(adj_ref, adj, in_sems.at[2])
    for copy in (cot_copy, mask_copy, adj_copy):
        copy.start()

    barrier = pltpu.get_barrier_semaphore()
    for partner in partners:
        pl.semaphore_signal(barrier, inc=1, device_id=partner, device_id_type=MESH)

    gb_ref[...] = jnp.zeros_like(gb_ref)
    cot_copy.wait()
    mask_copy.wait()

    def project(b, _):
        nodes = pl.ds(pl.multiple_of(b * BLK, BLK), BLK)
        grad = cot_ref[nodes, :].astype(F32) * mask_ref[nodes, :].astype(F32)
        grad16 = grad.astype(BF16)
        gpre[nodes, :] = grad16
        gb_ref[...] += jnp.sum(grad16.astype(F32), axis=0, keepdims=True)
        turned = lax.dot_general(weight_ref[...], grad16, (((1,), (1,)), ((), ())), preferred_element_type=F32)
        proj[col * SHARD + b] = turned.astype(BF16)
        return 0

    lax.fori_loop(0, SHARD, project, 0, unroll=SHARD)
    pl.semaphore_wait(barrier, len(partners))

    def part(buf, shard, half):
        return buf.at[pl.ds(shard * SHARD + half * HALF, HALF)]

    class Gather:
        def __init__(self, buf, own, shard, pos, pair, ring, mate):
            self.buf, self.own, self.shard, self.pos, self.pair, self.ring, self.mate = buf, own, shard, pos, pair, ring, mate
            self.l0 = [lines.line() for _ in range(2)]
            self.l1 = [[lines.line() for _ in range(2)] for _ in range(2)]
            self.l2 = [lines.line() for _ in range(2)]
            self.l3 = [[lines.line() for _ in range(2)] for _ in range(2)]
            self.l4 = [lines.line() for _ in range(2)]
            self.lf = lines.line()

        def place(self, pair_step, step, half):
            pair = self.pair if pair_step == 0 else 1 - self.pair
            return part(self.buf, self.shard(pair, (self.pos + step) % 4), half)

        def begin(self):
            for half in range(2):
                for d in range(2):
                    h = half if d == 0 else 1 - half
                    lines.send(self.l1[d][h], self.own(h), self.place(0, 0, h), self.ring(1 - 2 * d))
                lines.send(self.l0[half], self.own(half), self.place(0, 0, half), self.mate)

        def got_mate(self, h):
            lines.wait(self.l0[h], self.place(1, 0, h), self.mate)
            return self.place(1, 0, h)

        def pass_mate(self, h):
            for d in range(2):
                lines.send(self.l3[d][h], self.place(1, 0, h), self.place(1, 0, h), self.ring(1 - 2 * d))

        def got_ring(self, kind, d, h):
            step = 2 * d - 1
            table = self.l1 if kind == 0 else self.l3
            place = self.place(kind, step, h)
            lines.wait(table[d][h], place, self.ring(step))
            return place

        def pass_ring(self, kind, d):
            step = 2 * d - 1
            table = self.l2 if kind == 0 else self.l4
            place = self.place(kind, step, d)
            lines.send(table[d], place, place, self.ring(-step))

        def quarter(self, step, d):
            shard = self.shard(1 - self.pair, (self.pos + step) % 4)
            return self.buf.at[pl.ds(shard * SHARD + d * (HALF // 2), HALF // 2)]

        def pass_quarter(self, d):
            place = self.quarter(2 * d - 1, d)
            lines.send(self.l4[d], place, place, self.ring(1 - 2 * d))

        def got_quarter(self, d):
            lines.wait(self.l4[d], self.quarter(2, d), self.ring(2 * d - 1))

        def far_to_mate(self):
            place = self.place(0, 2, 1)
            lines.send(self.lf, place, place, self.mate)

        def far_from_mate(self):
            lines.wait(self.lf, self.place(1, 2, 1), self.mate)

        def got_far(self, kind, d):
            step = 2 * d - 1
            table = self.l2 if kind == 0 else self.l4
            place = self.place(kind, 2, d)
            lines.wait(table[d], place, self.ring(step))
            return place

    rows_g = Gather(feats, lambda h: feat_ref.at[pl.ds(h * HALF, HALF)],
                    lambda pair, pos: pair * 4 + pos, y, xh, at_y, pair_x)
    rows_g.begin()

    cols_g = Gather(proj, lambda h: part(proj, col, h),
                    lambda pair, pos: (pair * 4 + pos) * 2 + core, z, xl, at_z, near_x)
    cols_g.begin()

    across = []

    def cross(pair_step, step, h):
        line = lines.line()
        place = cols_g.place(pair_step, step, h)
        lines.send(line, place, place, other)
        pair = xl if pair_step == 0 else 1 - xl
        there = part(proj, (pair * 4 + (z + step) % 4) * 2 + 1 - core, h)
        across.append((line, there))

    feats[pl.ds(row * SHARD, SHARD)] = feat_ref[...]

    cross(0, 0, 0)
    cross(0, 0, 1)
    plan(count_ref, rows_ref, cols_ref, idx_vmem, flt_vmem)
    idx_copy = pltpu.make_async_copy(idx_vmem, idx_ref, in_sems.at[3])
    flt_copy = pltpu.make_async_copy(flt_vmem, flt_ref, in_sems.at[4])
    idx_copy.start()
    flt_copy.start()
    for d in range(2):
        rows_g.got_ring(0, d, d)
        rows_g.pass_ring(0, d)
    for d in range(2):
        cols_g.got_ring(0, d, d)
        cols_g.pass_ring(0, d)
    for h in range(2):
        rows_g.got_mate(h)
    for h in range(2):
        rows_g.pass_mate(h)
    for d in (1, 0):
        rows_g.got_far(0, d)
        if d == 1:
            rows_g.far_to_mate()
    for h in range(2):
        cols_g.got_mate(h)
        cols_g.pass_mate(h)
    for d in range(2):
        cross(0, 2 * d - 1, d)
        cross(1, 0, d)
    for d in range(2):
        cols_g.got_ring(0, d, 1 - d)
        cross(0, 2 * d - 1, 1 - d)
    for d in range(2):
        rows_g.got_ring(1, d, 0)
        rows_g.pass_quarter(d)
    for d in range(2):
        cols_g.got_far(0, d)
        cross(0, 2, d)
    for d in range(2):
        cols_g.got_ring(1, d, d)
        cols_g.pass_ring(1, d)
        cross(1, 2 * d - 1, d)
    for d in range(2):
        rows_g.got_ring(0, d, 1 - d)
        rows_g.got_ring(1, d, 1)
    for d in range(2):
        rows_g.got_quarter(d)
    rows_g.far_from_mate()
    adj_copy.wait()
    idx_copy.wait()
    flt_copy.wait()

    def spread(mates, source, target, place):
        used = [lines.line() for _ in mates]
        for line, (mate, theirs) in zip(used, mates):
            lines.send(line, source(theirs), target.at[place], mate)
        return used

    def collect(mates, used, target):
        for line, (mate, theirs) in zip(used, mates):
            lines.wait(line, target.at[theirs], mate)

    def added(ref):
        total = ref[0]
        for n in range(1, ref.shape[0]):
            total = total + ref[n]
        return total

    bias_own[0] = gb_ref[...]
    bias_col[col] = gb_ref[...]
    bias_lines = spread(col_mates, lambda theirs: bias_own.at[0], bias_col, col)

    slots = adj.shape[0]

    def forward(p, total):
        total = total * flt_ref[0, p] + jnp.dot(adj[idx_ref[0, p]], feats[idx_ref[1, p]], preferred_element_type=F32)
        run[p] = total
        return total

    lax.fori_loop(0, slots, forward, jnp.zeros((BLK, BLK), F32), unroll=64)

    def row_block(b):
        return run[idx_ref[2, b]] * flt_ref[1, b]

    order = [(1, 2), (1, 1), (1, -1), (0, 1), (0, -1), (0, 2), (1, 0), (0, 0)]

    def spot(pair, pos, step):
        return pair * 4 + (pos + step) % 4

    core_lines = {}
    for pair_step, step in order:
        q = spot(1 - xl if pair_step else xl, z, step)

        def fill(b, _, q=q):
            rsend[q * SHARD + b] = row_block((q * 2 + 1 - core) * SHARD + b).astype(BF16)
            return 0

        lax.fori_loop(0, SHARD, fill, 0, unroll=SHARD)
        line = core_lines[pair_step, step] = lines.line()
        place = pl.ds(q * SHARD, SHARD)
        lines.send(line, rsend.at[place], crecv.at[place], other)

    def add_core(pair_step, step):
        q = spot(1 - xl if pair_step else xl, z, step)
        lines.wait(core_lines[pair_step, step], crecv.at[pl.ds(q * SHARD, SHARD)], other)

        def fill(b, _):
            rown[q * SHARD + b] = row_block((q * 2 + core) * SHARD + b) + crecv[q * SHARD + b].astype(F32)
            return 0

        lax.fori_loop(0, SHARD, fill, 0, unroll=SHARD)

    class Scatter:
        def __init__(self, s1, r1, s2, r2, xs, xr, term, ring, mate, far_by_mate):
            self.s1, self.r1, self.s2, self.r2, self.xs, self.xr = s1, r1, s2, r2, xs, xr
            self.term, self.ring, self.mate, self.far_by_mate = term, ring, mate, far_by_mate
            self.l1 = [[lines.line() for _ in range(2)] for _ in range(2)]
            self.l2 = [[[lines.line() for _ in range(2)] for _ in range(2)] for _ in range(2)]
            self.lx = [lines.line() for _ in range(2)]

        def far(self, pair_step):
            for d in range(2):
                if self.far_by_mate and pair_step == 0:
                    lines.wait(self.l1[1][d], self.r1.at[pl.ds(SHARD + d * HALF, HALF)], self.mate)

                def fill(b, _, d=d):
                    b = d * HALF + b
                    value = self.term(pair_step, 2, b)
                    if self.far_by_mate and pair_step == 0:
                        value = value + self.r1[SHARD + b].astype(F32)
                    self.s1[pair_step * SHARD + b] = value.astype(BF16)
                    return 0

                lax.fori_loop(0, HALF, fill, 0, unroll=HALF)
                place = pl.ds(pair_step * SHARD + d * HALF, HALF)
                lines.send(self.l1[pair_step][d], self.s1.at[place], self.r1.at[place],
                           self.mate if self.far_by_mate and pair_step else self.ring(1 - 2 * d))

        def near(self, pair_step, d, late):
            h = d if late else 1 - d
            base = (pair_step * 2 + d) * SHARD + h * HALF
            passing = late and not (self.far_by_mate and pair_step)
            if passing:
                place = pl.ds(pair_step * SHARD + d * HALF, HALF)
                lines.wait(self.l1[pair_step][d], self.r1.at[place], self.ring(2 * d - 1))

            def fill(b, _):
                value = self.term(pair_step, 1 - 2 * d, h * HALF + b)
                if passing:
                    value = value + self.r1[pair_step * SHARD + d * HALF + b].astype(F32)
                self.s2[base + b] = value.astype(BF16)
                return 0

            lax.fori_loop(0, HALF, fill, 0, unroll=HALF)
            place = pl.ds(base, HALF)
            lines.send(self.l2[pair_step][d][h], self.s2.at[place], self.r2.at[place], self.ring(1 - 2 * d))

        def wait_near(self, pair_step, h):
            for d in range(2):
                place = pl.ds((pair_step * 2 + d) * SHARD + h * HALF, HALF)
                lines.wait(self.l2[pair_step][d][h], self.r2.at[place], self.ring(2 * d - 1))

        def total(self, pair_step, b):
            base = pair_step * 2 * SHARD + b
            return (self.term(pair_step, 0, b) + self.r2[base].astype(F32)) + self.r2[base + SHARD].astype(F32)

        def swap(self, h):
            self.wait_near(1, h)

            def fill(b, _):
                self.xs[h * HALF + b] = self.total(1, h * HALF + b).astype(BF16)
                return 0

            lax.fori_loop(0, HALF, fill, 0, unroll=HALF)
            place = pl.ds(h * HALF, HALF)
            lines.send(self.lx[h], self.xs.at[place], self.xr.at[place], self.mate)

        def finish(self, h, use):
            self.wait_near(0, h)
            lines.wait(self.lx[h], self.xr.at[pl.ds(h * HALF, HALF)], self.mate)

            def body(b, _):
                b = h * HALF + b
                use(b, self.total(0, b) + self.xr[b].astype(F32))
                return 0

            lax.fori_loop(0, HALF, body, 0, unroll=HALF)

    def row_term(pair_step, step, b):
        return rown[spot(1 - xl if pair_step else xl, z, step) * SHARD + b]

    rows_s = Scatter(zs1, zr1, zs2, zr2, zxs, zxr, row_term, at_z, near_x, True)
    add_core(1, 2)
    rows_s.far(1)
    for d in range(2):
        add_core(1, 1 - 2 * d)
        rows_s.near(1, d, False)
    for d in range(2):
        rows_s.near(1, d, True)
    for d in range(2):
        add_core(0, 1 - 2 * d)
        rows_s.near(0, d, False)
    add_core(0, 2)
    for pair_step in (1, 0):
        add_core(pair_step, 0)
    for d in range(2):
        cols_g.got_ring(1, d, 1 - d)
        cross(1, 2 * d - 1, 1 - d)
    for d in range(2):
        cols_g.got_far(1, d)
        cross(1, 2, d)

    for line, there in across:
        lines.wait(line, there, other)

    def backward(p, total):
        total = total * flt_ref[2, p] + jnp.dot(proj[idx_ref[4, p]], adj[idx_ref[3, p]], preferred_element_type=F32)
        run[p] = total
        return total

    lax.fori_loop(0, slots, backward, jnp.zeros((BLK, BLK), F32), unroll=32)

    def col_term(pair_step, step, b):
        at = spot(1 - xh if pair_step else xh, y, step) * SHARD + b
        return run[idx_ref[5, at]] * flt_ref[3, at]

    cols_s = Scatter(ys1, yr1, ys2, yr2, yxs, yxr, col_term, at_y, pair_x, False)
    cols_s.far(1)
    for d in range(2):
        cols_s.near(1, d, False)
    rows_s.far(0)
    for h in range(2):
        rows_s.swap(h)
    for d in range(2):
        cols_s.near(1, d, True)
    cols_s.far(0)
    for d in range(2):
        cols_s.near(0, d, False)
    for d in range(2):
        rows_s.near(0, d, True)

    collect(col_mates, bias_lines, bias_col)
    bias_row[row] = added(bias_col)
    bias_lines = spread(row_mates, lambda theirs: bias_row.at[row], bias_row, row)

    def aggregate(b, value):
        agg[b] = value.astype(BF16)

    def layer(b, _):
        nodes = pl.ds(pl.multiple_of(b * BLK, BLK), BLK)
        pre = jnp.dot(agg[b], weight_ref[...], preferred_element_type=F32) + bias_ref[...]
        out_ref[nodes, :] = (pre * mask_ref[nodes, :].astype(F32)).astype(BF16)
        return 0

    for h in range(2):
        rows_s.finish(h, aggregate)

    def weight_term(b, total):
        nodes = pl.ds(pl.multiple_of(b * BLK, BLK), BLK)
        return total + lax.dot_general(agg[b], gpre[nodes, :], (((0,), (0,)), ((), ())), preferred_element_type=F32)

    gw_ref[...] = lax.fori_loop(0, SHARD, weight_term, jnp.zeros(gw_ref.shape, F32), unroll=SHARD)

    pieces, depth = gsum.shape[0], gsum.shape[1]
    for n in range(pieces):
        gsum[n] = gw_ref[pl.ds(n * depth, depth), :]
    used = spread(col_mates, lambda theirs: gsum.at[theirs], ar_col, col)
    ar_col[col] = gsum[col]
    lax.fori_loop(0, SHARD, layer, 0, unroll=SHARD)
    for h in range(2):
        cols_s.swap(h)
    for d in range(2):
        cols_s.near(0, d, True)
    collect(col_mates, used, ar_col)
    ar_row[row] = added(ar_col)
    used = spread(row_mates, lambda theirs: ar_row.at[row], ar_row, row)
    collect(row_mates, used, ar_row)
    gall[col] = added(ar_row)
    used = spread(col_mates, lambda theirs: gall.at[col], gall, col)

    def store(b, value):
        gf_ref[b] = jnp.transpose(value).astype(BF16)

    for h in range(2):
        cols_s.finish(h, store)

    collect(row_mates, bias_lines, bias_row)
    gb_ref[...] = added(bias_row)
    collect(col_mates, used, gall)
    for n in range(pieces):
        gw_ref[pl.ds(n * depth, depth), :] = gall[n]
    lines.drain()
    assert lines.used <= N_LINES


def local(features, weight, bias, adjacency, block_rows, block_cols, block_count, cotangent, relu_mask):
    slots = adjacency.shape[2]
    vmem, smem, hbm = (pl.BlockSpec(memory_space=m) for m in (pltpu.VMEM, pltpu.SMEM, pl.ANY))
    hid = weight.shape[1]

    def blocks(n, dtype=BF16):
        return pltpu.VMEM((n, BLK, BLK), dtype)

    plan_shape = (8, slots)
    scratch = [
        pltpu.VMEM(plan_shape, jnp.int32), pltpu.VMEM(plan_shape, F32), pltpu.SMEM(plan_shape, jnp.int32), pltpu.SMEM(plan_shape, F32),
        pltpu.VMEM((1024, hid), BF16), pltpu.VMEM((1024, hid), jnp.int32),
        blocks(slots), blocks(slots, F32), blocks(64), blocks(128), pltpu.VMEM((1024, hid), BF16),
        blocks(64), blocks(64), blocks(64, F32)]
    for _ in range(2):
        scratch += [blocks(16), blocks(16), blocks(32), blocks(32), blocks(8), blocks(8)]
    piece = (8, hid)
    scratch += [blocks(8)] + [pltpu.VMEM((n,) + piece, F32) for n in (16, 16, 8, 16)]
    scratch += [pltpu.VMEM((n, 1, hid), F32) for n in (1, 16, 8)]
    scratch += [pltpu.SemaphoreType.DMA((N_LINES,)), pltpu.SemaphoreType.DMA((N_LINES,)), pltpu.SemaphoreType.DMA((5,))]
    out, gf, gw, gb = pl.pallas_call(
        layer_kernel,
        out_shape=(
            jax.ShapeDtypeStruct((1024, hid), BF16),
            jax.ShapeDtypeStruct((SHARD, BLK, BLK), BF16),
            jax.ShapeDtypeStruct(weight.shape, F32),
            jax.ShapeDtypeStruct((1, hid), F32),
        ),
        in_specs=[smem, vmem, vmem, vmem, vmem, vmem, hbm, hbm, hbm],
        out_specs=(vmem, vmem, vmem, vmem),
        scratch_shapes=scratch,
        compiler_params=pltpu.CompilerParams(collective_id=0, has_side_effects=True, vmem_limit_bytes=51 * 2**20),
        name="layer",
    )(block_count, block_rows[0], block_cols[0], features.reshape(SHARD, BLK, BLK), weight, bias.reshape(1, hid), cotangent, relu_mask,
      adjacency.reshape(slots, BLK, BLK))
    results = (out, gf, gw, gb)
    out, gf, gw, gb = pl.pallas_call(
        hand_on_kernel,
        out_shape=tuple(jax.ShapeDtypeStruct(r.shape, r.dtype) for r in results),
        in_specs=[vmem] * 4,
        out_specs=(vmem,) * 4,
        name="hand_on",
    )(*results)
    return out, gf.reshape(1024, BLK), gw, gb.reshape(hid)


def solution(mesh):
    in_specs = (
        P(("col", "row"), None),
        P(),
        P(),
        P("row", "col", None, None, None),
        P("row", "col", None),
        P("row", "col", None),
        P("row", "col"),
        P(("row", "col"), None),
        P(("row", "col"), None),
    )
    out_specs = (P(("row", "col"), None), P(("col", "row"), None), P(), P())
    return jax.shard_map(local, mesh=mesh, in_specs=in_specs, out_specs=out_specs, check_vma=False)
```

```python
import functools

import jax
import jax.numpy as jnp
from jax import lax
from jax.experimental import pallas as pl
from jax.experimental.pallas import tpu as pltpu
from jax.sharding import PartitionSpec as P

F32 = jnp.float32
BF16 = jnp.bfloat16
MESH = pl.DeviceIdType.MESH
BLK = 128
SHARD = 8
HALF = 4


def plan(count_ref, rows_ref, cols_ref, idx_ref, flt_ref):
    n = rows_ref.shape[1]
    count = count_ref[0, 0]
    lane = lax.broadcasted_iota(jnp.int32, (n, n), 1)
    sub = lax.broadcasted_iota(jnp.int32, (n, n), 0)
    one, zero = jnp.ones((n, n), jnp.int32), jnp.zeros((n, n), jnp.int32)
    eye = lane == sub
    live_l, live_c = lane < count, sub < count
    row_l = jnp.broadcast_to(rows_ref[...], (n, n))
    col_l = jnp.broadcast_to(cols_ref[...], (n, n))
    row_c = jnp.broadcast_to(jnp.sum(jnp.where(eye, row_l, zero), axis=1, keepdims=True), (n, n))
    col_c = jnp.broadcast_to(jnp.sum(jnp.where(eye, col_l, zero), axis=1, keepdims=True), (n, n))
    idx_ref[...] = jnp.zeros_like(idx_ref)
    flt_ref[...] = jnp.zeros_like(flt_ref)
    tops = (127, 63)
    for side, (major_l, major_c, minor_c) in enumerate(((row_l, row_c, col_c), (col_l, col_c, row_c))):
        far = jnp.full((n, n), 65536, jnp.int32)
        key_l = jnp.where(live_l, major_l * n, far) + lane
        key_c = jnp.where(live_c, major_c * n, far) + sub
        rank = jnp.sum(jnp.where(key_l < key_c, one, zero), axis=1, keepdims=True)
        hot = jnp.broadcast_to(rank, (n, n)) == lane
        same = jnp.where((major_l == major_c) & (lane < sub) & live_l, one, zero)
        keep = jnp.broadcast_to(jnp.minimum(jnp.sum(same, axis=1, keepdims=True), 1), (n, n))
        slot = jnp.sum(jnp.where(hot, sub, zero), axis=0, keepdims=True)
        minor = jnp.sum(jnp.where(hot, minor_c, zero), axis=0, keepdims=True)
        keep_sorted = jnp.sum(jnp.where(hot, keep, zero), axis=0, keepdims=True)
        upto = jnp.sum(jnp.where((major_c <= lane) & live_c, one, zero), axis=0, keepdims=True)
        here = jnp.sum(jnp.where((major_c == lane) & live_c, one, zero), axis=0, keepdims=True)
        idx_ref[3 * side : 3 * side + 1, :] = jnp.clip(slot, 0, n - 1)
        idx_ref[3 * side + 1 : 3 * side + 2, :] = jnp.clip(minor, 0, tops[1 - side])
        idx_ref[3 * side + 2 : 3 * side + 3, :] = jnp.clip(upto - 1, 0, n - 1)
        flt_ref[2 * side : 2 * side + 1, :] = keep_sorted.astype(F32)
        flt_ref[2 * side + 1 : 2 * side + 2, :] = jnp.minimum(here, 1).astype(F32)


def hand_on_kernel(*refs):
    half = len(refs) // 2
    for source, target in zip(refs[:half], refs[half:]):
        target[...] = source[...]


class Lines:
    def __init__(self, send_sems, recv_sems):
        self.send_sems, self.recv_sems, self.used, self.sent = send_sems, recv_sems, 0, []

    def line(self):
        self.used += 1
        return self.used - 1

    def send(self, line, src, dst, device):
        copy = pltpu.make_async_remote_copy(
            src_ref=src, dst_ref=dst, send_sem=self.send_sems.at[line], recv_sem=self.recv_sems.at[line],
            device_id=device, device_id_type=MESH)
        copy.start()
        self.sent.append(copy)

    def wait(self, line, dst, device):
        pltpu.make_async_remote_copy(
            src_ref=dst, dst_ref=dst, send_sem=self.send_sems.at[line], recv_sem=self.recv_sems.at[line],
            device_id=device, device_id_type=MESH).wait_recv()

    def drain(self):
        for copy in self.sent:
            copy.wait_send()


N_LINES = 160


def layer_kernel(
    count_ref, rows_hbm, cols_hbm, feat_hbm, weight_hbm, bias_hbm, cot_hbm, mask_hbm, adj_ref,
    out_hbm, gf_hbm, gw_hbm, gb_hbm,
    rows_ref, cols_ref, weight_ref, bias_ref, out_ref, gf_ref, gw_ref, gb_ref,
    idx_vmem, flt_vmem, idx_ref, flt_ref, cot_ref, mask_ref, adj, run, feats, proj, gpre, rsend, crecv, rown,
    zs1, zr1, zs2, zr2, zxs, zxr, ys1, yr1, ys2, yr2, yxs, yxr,
    agg, gsum, ar_col, ar_row, gall, bias_own, bias_col, bias_row,
    send_sems, recv_sems, in_sems):
    row, col = lax.axis_index("row"), lax.axis_index("col")
    xh, y = row // 4, row % 4
    xl, z, core = col // 8, (col // 2) % 4, col % 2
    lines = Lines(send_sems, recv_sems)

    def dev(xh=xh, y=y, xl=xl, z=z, core=core):
        return (xh * 4 + y, (xl * 4 + z) * 2 + core)

    def at_y(step):
        return dev(y=(y + step) % 4)

    def at_z(step):
        return dev(z=(z + step) % 4)

    pair_x = dev(xh=1 - xh)
    near_x = dev(xl=1 - xl)
    other = dev(core=1 - core)
    col_mates, row_mates = [], []
    for flip in (1, 0):
        for step in (2, 1, 3, 0):
            for turn in (1, 0):
                if flip or step or turn:
                    to_xl, to_z, to_core = (xl + flip) % 2, (z + step) % 4, (core + turn) % 2
                    col_mates.append((dev(xl=to_xl, z=to_z, core=to_core), (to_xl * 4 + to_z) * 2 + to_core))
            if flip or step:
                to_xh, to_y = (xh + flip) % 2, (y + step) % 4
                row_mates.append((dev(xh=to_xh, y=to_y), to_xh * 4 + to_y))
    partners = [mate for mate, _ in row_mates + col_mates]
    feat_copy = pltpu.make_async_copy(feat_hbm, feats.at[pl.ds(row * SHARD, SHARD)], in_sems.at[5])
    weight_copy = pltpu.make_async_copy(weight_hbm, weight_ref, in_sems.at[6])
    cot_copy = pltpu.make_async_copy(cot_hbm, cot_ref, in_sems.at[0])
    mask_copy = pltpu.make_async_copy(mask_hbm, mask_ref, in_sems.at[1])
    rows_copy = pltpu.make_async_copy(rows_hbm, rows_ref, in_sems.at[8])
    cols_copy = pltpu.make_async_copy(cols_hbm, cols_ref, in_sems.at[9])
    bias_copy = pltpu.make_async_copy(bias_hbm, bias_ref, in_sems.at[7])
    adj_copy = pltpu.make_async_copy(adj_ref, adj, in_sems.at[2])

    barrier = pltpu.get_barrier_semaphore()
    for partner in partners:
        pl.semaphore_signal(barrier, inc=1, device_id=partner, device_id_type=MESH)
    for copy in (cot_copy, mask_copy, weight_copy, feat_copy, rows_copy, cols_copy, bias_copy, adj_copy):
        copy.start()

    gb_ref[...] = jnp.zeros_like(gb_ref)
    weight_copy.wait()
    cot_copy.wait()
    mask_copy.wait()

    def project(b, _):
        nodes = pl.ds(pl.multiple_of(b * BLK, BLK), BLK)
        grad = cot_ref[nodes, :].astype(F32) * mask_ref[nodes, :].astype(F32)
        grad16 = grad.astype(BF16)
        gpre[nodes, :] = grad16
        gb_ref[...] += jnp.sum(grad16.astype(F32), axis=0, keepdims=True)
        turned = lax.dot_general(weight_ref[...], grad16, (((1,), (1,)), ((), ())), preferred_element_type=F32)
        proj[col * SHARD + b] = turned.astype(BF16)
        return 0

    lax.fori_loop(0, SHARD, project, 0, unroll=SHARD)
    pl.semaphore_wait(barrier, len(partners))

    def part(buf, shard, half):
        return buf.at[pl.ds(shard * SHARD + half * HALF, HALF)]

    class Gather:
        def __init__(self, buf, own, shard, pos, pair, ring, mate):
            self.buf, self.own, self.shard, self.pos, self.pair, self.ring, self.mate = buf, own, shard, pos, pair, ring, mate
            self.l0 = [lines.line() for _ in range(2)]
            self.l1 = [[lines.line() for _ in range(2)] for _ in range(2)]
            self.l2 = [lines.line() for _ in range(2)]
            self.l3 = [[lines.line() for _ in range(2)] for _ in range(2)]
            self.l4 = [lines.line() for _ in range(2)]
            self.lf = lines.line()

        def place(self, pair_step, step, half):
            pair = self.pair if pair_step == 0 else 1 - self.pair
            return part(self.buf, self.shard(pair, (self.pos + step) % 4), half)

        def begin(self):
            for half in range(2):
                for d in range(2):
                    h = half if d == 0 else 1 - half
                    lines.send(self.l1[d][h], self.own(h), self.place(0, 0, h), self.ring(1 - 2 * d))
                lines.send(self.l0[half], self.own(half), self.place(0, 0, half), self.mate)

        def got_mate(self, h):
            lines.wait(self.l0[h], self.place(1, 0, h), self.mate)
            return self.place(1, 0, h)

        def pass_mate(self, h):
            for d in range(2):
                lines.send(self.l3[d][h], self.place(1, 0, h), self.place(1, 0, h), self.ring(1 - 2 * d))

        def got_ring(self, kind, d, h):
            step = 2 * d - 1
            table = self.l1 if kind == 0 else self.l3
            place = self.place(kind, step, h)
            lines.wait(table[d][h], place, self.ring(step))
            return place

        def pass_ring(self, kind, d):
            step = 2 * d - 1
            table = self.l2 if kind == 0 else self.l4
            place = self.place(kind, step, d)
            lines.send(table[d], place, place, self.ring(-step))

        def quarter(self, step, d):
            shard = self.shard(1 - self.pair, (self.pos + step) % 4)
            return self.buf.at[pl.ds(shard * SHARD + d * (HALF // 2), HALF // 2)]

        def pass_quarter(self, d):
            place = self.quarter(2 * d - 1, d)
            lines.send(self.l4[d], place, place, self.ring(1 - 2 * d))

        def got_quarter(self, d):
            lines.wait(self.l4[d], self.quarter(2, d), self.ring(2 * d - 1))

        def far_to_mate(self):
            place = self.place(0, 2, 1)
            lines.send(self.lf, place, place, self.mate)

        def far_from_mate(self):
            lines.wait(self.lf, self.place(1, 2, 1), self.mate)

        def got_far(self, kind, d):
            step = 2 * d - 1
            table = self.l2 if kind == 0 else self.l4
            place = self.place(kind, 2, d)
            lines.wait(table[d], place, self.ring(step))
            return place

    feat_copy.wait()
    rows_g = Gather(feats, lambda h: part(feats, row, h),
                    lambda pair, pos: pair * 4 + pos, y, xh, at_y, pair_x)
    rows_g.begin()

    cols_g = Gather(proj, lambda h: part(proj, col, h),
                    lambda pair, pos: (pair * 4 + pos) * 2 + core, z, xl, at_z, near_x)
    cols_g.begin()

    across = []

    def cross(pair_step, step, h):
        line = lines.line()
        place = cols_g.place(pair_step, step, h)
        lines.send(line, place, place, other)
        pair = xl if pair_step == 0 else 1 - xl
        there = part(proj, (pair * 4 + (z + step) % 4) * 2 + 1 - core, h)
        across.append((line, there))

    cross(0, 0, 0)
    cross(0, 0, 1)
    for copy in (rows_copy, cols_copy, bias_copy):
        copy.wait()
    plan(count_ref, rows_ref, cols_ref, idx_vmem, flt_vmem)
    idx_copy = pltpu.make_async_copy(idx_vmem, idx_ref, in_sems.at[3])
    flt_copy = pltpu.make_async_copy(flt_vmem, flt_ref, in_sems.at[4])
    idx_copy.start()
    flt_copy.start()
    for d in range(2):
        rows_g.got_ring(0, d, d)
        rows_g.pass_ring(0, d)
    for d in range(2):
        cols_g.got_ring(0, d, d)
        cols_g.pass_ring(0, d)
    for h in range(2):
        rows_g.got_mate(h)
    for h in range(2):
        rows_g.pass_mate(h)
    for d in (1, 0):
        rows_g.got_far(0, d)
        if d == 1:
            rows_g.far_to_mate()
    for h in range(2):
        cols_g.got_mate(h)
        cols_g.pass_mate(h)
    for d in range(2):
        cross(0, 2 * d - 1, d)
        cross(1, 0, d)
    for d in range(2):
        cols_g.got_ring(0, d, 1 - d)
        cross(0, 2 * d - 1, 1 - d)
    for d in range(2):
        rows_g.got_ring(1, d, 0)
        rows_g.pass_quarter(d)
    for d in range(2):
        cols_g.got_far(0, d)
        cross(0, 2, d)
    for d in range(2):
        cols_g.got_ring(1, d, d)
        cols_g.pass_ring(1, d)
        cross(1, 2 * d - 1, d)
    for d in range(2):
        rows_g.got_ring(0, d, 1 - d)
        rows_g.got_ring(1, d, 1)
    for d in range(2):
        rows_g.got_quarter(d)
    rows_g.far_from_mate()
    adj_copy.wait()
    idx_copy.wait()
    flt_copy.wait()

    def spread(mates, source, target, place):
        used = [lines.line() for _ in mates]
        for line, (mate, theirs) in zip(used, mates):
            lines.send(line, source(theirs), target.at[place], mate)
        return used

    def collect(mates, used, target):
        for line, (mate, theirs) in zip(used, mates):
            lines.wait(line, target.at[theirs], mate)

    def added(ref):
        total = ref[0]
        for n in range(1, ref.shape[0]):
            total = total + ref[n]
        return total

    bias_own[0] = gb_ref[...]
    bias_col[col] = gb_ref[...]
    bias_lines = spread(col_mates, lambda theirs: bias_own.at[0], bias_col, col)

    slots = adj.shape[0]

    def forward(p, total):
        total = total * flt_ref[0, p] + jnp.dot(adj[idx_ref[0, p]], feats[idx_ref[1, p]], preferred_element_type=F32)
        run[p] = total
        return total

    lax.fori_loop(0, slots, forward, jnp.zeros((BLK, BLK), F32), unroll=64)

    def row_block(b):
        return run[idx_ref[2, b]] * flt_ref[1, b]

    order = [(1, 2), (1, 1), (1, -1), (0, 1), (0, -1), (0, 2), (1, 0), (0, 0)]

    def spot(pair, pos, step):
        return pair * 4 + (pos + step) % 4

    core_lines = {}
    for pair_step, step in order:
        q = spot(1 - xl if pair_step else xl, z, step)

        def fill(b, _, q=q):
            rsend[q * SHARD + b] = row_block((q * 2 + 1 - core) * SHARD + b).astype(BF16)
            return 0

        lax.fori_loop(0, SHARD, fill, 0, unroll=SHARD)
        line = core_lines[pair_step, step] = lines.line()
        place = pl.ds(q * SHARD, SHARD)
        lines.send(line, rsend.at[place], crecv.at[place], other)

    def add_core(pair_step, step):
        q = spot(1 - xl if pair_step else xl, z, step)
        lines.wait(core_lines[pair_step, step], crecv.at[pl.ds(q * SHARD, SHARD)], other)

        def fill(b, _):
            rown[q * SHARD + b] = row_block((q * 2 + core) * SHARD + b) + crecv[q * SHARD + b].astype(F32)
            return 0

        lax.fori_loop(0, SHARD, fill, 0, unroll=SHARD)

    class Scatter:
        def __init__(self, s1, r1, s2, r2, xs, xr, term, ring, mate, far_by_mate):
            self.s1, self.r1, self.s2, self.r2, self.xs, self.xr = s1, r1, s2, r2, xs, xr
            self.term, self.ring, self.mate, self.far_by_mate = term, ring, mate, far_by_mate
            self.l1 = [[lines.line() for _ in range(2)] for _ in range(2)]
            self.l2 = [[[lines.line() for _ in range(2)] for _ in range(2)] for _ in range(2)]
            self.l2b = [lines.line() for _ in range(2)]
            self.lx = [lines.line() for _ in range(2)]

        def far(self, pair_step, ways=(0, 1)):
            for d in ways:
                if self.far_by_mate and pair_step == 0:
                    lines.wait(self.l1[1][d], self.r1.at[pl.ds(SHARD + d * HALF, HALF)], self.mate)

                def fill(b, _, d=d):
                    b = d * HALF + b
                    value = self.term(pair_step, 2, b)
                    if self.far_by_mate and pair_step == 0:
                        value = value + self.r1[SHARD + b].astype(F32)
                    self.s1[pair_step * SHARD + b] = value.astype(BF16)
                    return 0

                lax.fori_loop(0, HALF, fill, 0, unroll=HALF)
                place = pl.ds(pair_step * SHARD + d * HALF, HALF)
                lines.send(self.l1[pair_step][d], self.s1.at[place], self.r1.at[place],
                           self.mate if self.far_by_mate and pair_step else self.ring(1 - 2 * d))

        def near(self, pair_step, d, late, cut=None):
            h = d if late else 1 - d
            first = h * HALF + (cut or 0) * (HALF // 2)
            count = HALF if cut is None else HALF // 2
            base = (pair_step * 2 + d) * SHARD + first
            line = self.l2b[d] if cut else self.l2[pair_step][d][h]
            passing = late and not (self.far_by_mate and pair_step)
            if passing:
                place = pl.ds(pair_step * SHARD + d * HALF, HALF)
                lines.wait(self.l1[pair_step][d], self.r1.at[place], self.ring(2 * d - 1))

            def fill(b, _):
                value = self.term(pair_step, 1 - 2 * d, first + b)
                if passing:
                    value = value + self.r1[pair_step * SHARD + d * HALF + b].astype(F32)
                self.s2[base + b] = value.astype(BF16)
                return 0

            lax.fori_loop(0, count, fill, 0, unroll=count)
            place = pl.ds(base, count)
            lines.send(line, self.s2.at[place], self.r2.at[place], self.ring(1 - 2 * d))

        def wait_near(self, pair_step, h):
            for d in range(2):
                base = (pair_step * 2 + d) * SHARD + h * HALF
                if pair_step == 0 and h == 1 - d:
                    for cut, line in enumerate((self.l2[0][d][h], self.l2b[d])):
                        lines.wait(line, self.r2.at[pl.ds(base + cut * (HALF // 2), HALF // 2)], self.ring(2 * d - 1))
                else:
                    lines.wait(self.l2[pair_step][d][h], self.r2.at[pl.ds(base, HALF)], self.ring(2 * d - 1))

        def total(self, pair_step, b):
            base = pair_step * 2 * SHARD + b
            return (self.term(pair_step, 0, b) + self.r2[base].astype(F32)) + self.r2[base + SHARD].astype(F32)

        def swap(self, h):
            self.wait_near(1, h)

            def fill(b, _):
                self.xs[h * HALF + b] = self.total(1, h * HALF + b).astype(BF16)
                return 0

            lax.fori_loop(0, HALF, fill, 0, unroll=HALF)
            place = pl.ds(h * HALF, HALF)
            lines.send(self.lx[h], self.xs.at[place], self.xr.at[place], self.mate)

        def finish(self, h, use):
            self.wait_near(0, h)
            lines.wait(self.lx[h], self.xr.at[pl.ds(h * HALF, HALF)], self.mate)

            def body(b, _):
                b = h * HALF + b
                use(b, self.total(0, b) + self.xr[b].astype(F32))
                return 0

            lax.fori_loop(0, HALF, body, 0, unroll=HALF)

    def row_term(pair_step, step, b):
        return rown[spot(1 - xl if pair_step else xl, z, step) * SHARD + b]

    rows_s = Scatter(zs1, zr1, zs2, zr2, zxs, zxr, row_term, at_z, near_x, True)
    add_core(1, 2)
    rows_s.far(1)
    for d in range(2):
        add_core(1, 1 - 2 * d)
        rows_s.near(1, d, False)
    for d in range(2):
        rows_s.near(1, d, True)
    for d in range(2):
        add_core(0, 1 - 2 * d)
        rows_s.near(0, d, False, 0)
    add_core(0, 2)
    for pair_step in (1, 0):
        add_core(pair_step, 0)
    for d in range(2):
        cols_g.got_ring(1, d, 1 - d)
        cross(1, 2 * d - 1, 1 - d)
    for d in range(2):
        cols_g.got_far(1, d)
        cross(1, 2, d)

    for line, there in across:
        lines.wait(line, there, other)

    def backward(p, total):
        total = total * flt_ref[2, p] + jnp.dot(proj[idx_ref[4, p]], adj[idx_ref[3, p]], preferred_element_type=F32)
        run[p] = total
        return total

    lax.fori_loop(0, slots, backward, jnp.zeros((BLK, BLK), F32), unroll=32)

    def col_term(pair_step, step, b):
        at = spot(1 - xh if pair_step else xh, y, step) * SHARD + b
        return run[idx_ref[5, at]] * flt_ref[3, at]

    cols_s = Scatter(ys1, yr1, ys2, yr2, yxs, yxr, col_term, at_y, pair_x, False)
    cols_s.far(1)
    for d in range(2):
        cols_s.near(1, d, False)
    for d in range(2):
        rows_s.far(0, (d,))
        rows_s.near(0, d, False, 1)
    for h in range(2):
        rows_s.swap(h)
    for d in range(2):
        cols_s.near(1, d, True)
    cols_s.far(0)
    for d in range(2):
        for cut in range(2):
            cols_s.near(0, d, False, cut)
    for d in range(2):
        rows_s.near(0, d, True)

    collect(col_mates, bias_lines, bias_col)
    bias_row[row] = added(bias_col)
    bias_lines = spread(row_mates, lambda theirs: bias_row.at[row], bias_row, row)

    def aggregate(b, value):
        agg[b] = value.astype(BF16)

    def layer(b, _):
        nodes = pl.ds(pl.multiple_of(b * BLK, BLK), BLK)
        pre = jnp.dot(agg[b], weight_ref[...], preferred_element_type=F32) + bias_ref[...]
        out_ref[nodes, :] = (pre * mask_ref[nodes, :].astype(F32)).astype(BF16)
        return 0

    for h in range(2):
        rows_s.finish(h, aggregate)

    def weight_term(b, total):
        nodes = pl.ds(pl.multiple_of(b * BLK, BLK), BLK)
        return total + lax.dot_general(agg[b], gpre[nodes, :], (((0,), (0,)), ((), ())), preferred_element_type=F32)

    gw_ref[...] = lax.fori_loop(0, SHARD, weight_term, jnp.zeros(gw_ref.shape, F32), unroll=SHARD)

    pieces, depth = gsum.shape[0], gsum.shape[1]
    for n in range(pieces):
        gsum[n] = gw_ref[pl.ds(n * depth, depth), :]
    used = spread(col_mates, lambda theirs: gsum.at[theirs], ar_col, col)
    ar_col[col] = gsum[col]
    lax.fori_loop(0, SHARD, layer, 0, unroll=SHARD)
    out_copy = pltpu.make_async_copy(out_ref, out_hbm, in_sems.at[10])
    out_copy.start()
    for h in range(2):
        cols_s.swap(h)
    for d in range(2):
        cols_s.near(0, d, True)
    collect(col_mates, used, ar_col)
    ar_row[row] = added(ar_col)
    used = spread(row_mates, lambda theirs: ar_row.at[row], ar_row, row)
    collect(row_mates, used, ar_row)
    gall[col] = added(ar_row)
    used = spread(col_mates, lambda theirs: gall.at[col], gall, col)

    def store(b, value):
        gf_ref[b] = jnp.transpose(value).astype(BF16)

    for h in range(2):
        cols_s.finish(h, store)
    gf_copy = pltpu.make_async_copy(gf_ref, gf_hbm, in_sems.at[11])
    gf_copy.start()

    collect(row_mates, bias_lines, bias_row)
    gb_ref[...] = added(bias_row)
    collect(col_mates, used, gall)
    for n in range(pieces):
        gw_ref[pl.ds(n * depth, depth), :] = gall[n]
    gw_copy = pltpu.make_async_copy(gw_ref, gw_hbm, in_sems.at[12])
    gb_copy = pltpu.make_async_copy(gb_ref, gb_hbm, in_sems.at[13])
    gw_copy.start()
    gb_copy.start()
    lines.drain()
    for copy in (out_copy, gf_copy, gw_copy, gb_copy):
        copy.wait()
    assert lines.used <= N_LINES


def local(features, weight, bias, adjacency, block_rows, block_cols, block_count, cotangent, relu_mask):
    slots = adjacency.shape[2]
    vmem, smem, hbm = (pl.BlockSpec(memory_space=m) for m in (pltpu.VMEM, pltpu.SMEM, pl.ANY))
    hid = weight.shape[1]

    def blocks(n, dtype=BF16):
        return pltpu.VMEM((n, BLK, BLK), dtype)

    plan_shape = (8, slots)
    scratch = [
        pltpu.VMEM((1, slots), jnp.int32), pltpu.VMEM((1, slots), jnp.int32), pltpu.VMEM(weight.shape, BF16), pltpu.VMEM((1, hid), F32),
        pltpu.VMEM((1024, hid), BF16), pltpu.VMEM((SHARD, BLK, BLK), BF16), pltpu.VMEM(weight.shape, F32), pltpu.VMEM((1, hid), F32),
        pltpu.VMEM(plan_shape, jnp.int32), pltpu.VMEM(plan_shape, F32), pltpu.SMEM(plan_shape, jnp.int32), pltpu.SMEM(plan_shape, F32),
        pltpu.VMEM((1024, hid), BF16), pltpu.VMEM((1024, hid), jnp.int32),
        blocks(slots), blocks(slots, F32), blocks(64), blocks(128), pltpu.VMEM((1024, hid), BF16),
        blocks(64), blocks(64), blocks(64, F32)]
    for _ in range(2):
        scratch += [blocks(16), blocks(16), blocks(32), blocks(32), blocks(8), blocks(8)]
    piece = (8, hid)
    scratch += [blocks(8)] + [pltpu.VMEM((n,) + piece, F32) for n in (16, 16, 8, 16)]
    scratch += [pltpu.VMEM((n, 1, hid), F32) for n in (1, 16, 8)]
    scratch += [pltpu.SemaphoreType.DMA((N_LINES,)), pltpu.SemaphoreType.DMA((N_LINES,)), pltpu.SemaphoreType.DMA((14,))]
    out, gf, gw, gb = pl.pallas_call(
        layer_kernel,
        out_shape=(
            jax.ShapeDtypeStruct((1024, hid), BF16),
            jax.ShapeDtypeStruct((SHARD, BLK, BLK), BF16),
            jax.ShapeDtypeStruct(weight.shape, F32),
            jax.ShapeDtypeStruct((1, hid), F32),
        ),
        in_specs=[smem] + [hbm] * 8,
        out_specs=(hbm,) * 4,
        scratch_shapes=scratch,
        compiler_params=pltpu.CompilerParams(collective_id=0, has_side_effects=True, vmem_limit_bytes=60 * 2**20),
        name="layer",
    )(block_count, block_rows[0], block_cols[0], features.reshape(SHARD, BLK, BLK), weight, bias.reshape(1, hid), cotangent, relu_mask,
      adjacency.reshape(slots, BLK, BLK))
    results = (out, gf, gw, gb)
    out, gf, gw, gb = pl.pallas_call(
        hand_on_kernel,
        out_shape=tuple(jax.ShapeDtypeStruct(r.shape, r.dtype) for r in results),
        in_specs=[vmem] * 4,
        out_specs=(vmem,) * 4,
        name="hand_on",
    )(*results)
    return out, gf.reshape(1024, BLK), gw, gb.reshape(hid)


def solution(mesh):
    in_specs = (
        P(("col", "row"), None),
        P(),
        P(),
        P("row", "col", None, None, None),
        P("row", "col", None),
        P("row", "col", None),
        P("row", "col"),
        P(("row", "col"), None),
        P(("row", "col"), None),
    )
    out_specs = (P(("row", "col"), None), P(("col", "row"), None), P(), P())
    return jax.shard_map(local, mesh=mesh, in_specs=in_specs, out_specs=out_specs, check_vma=False)
```

```python
import functools

import jax
import jax.numpy as jnp
from jax import lax
from jax.experimental import pallas as pl
from jax.experimental.pallas import tpu as pltpu
from jax.sharding import PartitionSpec as P

F32 = jnp.float32
BF16 = jnp.bfloat16
MESH = pl.DeviceIdType.MESH
BLK = 128
SHARD = 8
HALF = 4


def plan(count_ref, rows_ref, cols_ref, idx_ref, flt_ref):
    n = rows_ref.shape[1]
    count = count_ref[0, 0]
    lane = lax.broadcasted_iota(jnp.int32, (n, n), 1)
    sub = lax.broadcasted_iota(jnp.int32, (n, n), 0)
    one, zero = jnp.ones((n, n), jnp.int32), jnp.zeros((n, n), jnp.int32)
    eye = lane == sub
    live_l, live_c = lane < count, sub < count
    row_l = jnp.broadcast_to(rows_ref[...], (n, n))
    col_l = jnp.broadcast_to(cols_ref[...], (n, n))
    row_c = jnp.broadcast_to(jnp.sum(jnp.where(eye, row_l, zero), axis=1, keepdims=True), (n, n))
    col_c = jnp.broadcast_to(jnp.sum(jnp.where(eye, col_l, zero), axis=1, keepdims=True), (n, n))
    idx_ref[...] = jnp.zeros_like(idx_ref)
    flt_ref[...] = jnp.zeros_like(flt_ref)
    tops = (127, 63)
    for side, (major_l, major_c, minor_c) in enumerate(((row_l, row_c, col_c), (col_l, col_c, row_c))):
        far = jnp.full((n, n), 65536, jnp.int32)
        key_l = jnp.where(live_l, major_l * n, far) + lane
        key_c = jnp.where(live_c, major_c * n, far) + sub
        rank = jnp.sum(jnp.where(key_l < key_c, one, zero), axis=1, keepdims=True)
        hot = jnp.broadcast_to(rank, (n, n)) == lane
        same = jnp.where((major_l == major_c) & (lane < sub) & live_l, one, zero)
        keep = jnp.broadcast_to(jnp.minimum(jnp.sum(same, axis=1, keepdims=True), 1), (n, n))
        slot = jnp.sum(jnp.where(hot, sub, zero), axis=0, keepdims=True)
        minor = jnp.sum(jnp.where(hot, minor_c, zero), axis=0, keepdims=True)
        keep_sorted = jnp.sum(jnp.where(hot, keep, zero), axis=0, keepdims=True)
        upto = jnp.sum(jnp.where((major_c <= lane) & live_c, one, zero), axis=0, keepdims=True)
        here = jnp.sum(jnp.where((major_c == lane) & live_c, one, zero), axis=0, keepdims=True)
        idx_ref[3 * side : 3 * side + 1, :] = jnp.clip(slot, 0, n - 1)
        idx_ref[3 * side + 1 : 3 * side + 2, :] = jnp.clip(minor, 0, tops[1 - side])
        idx_ref[3 * side + 2 : 3 * side + 3, :] = jnp.clip(upto - 1, 0, n - 1)
        flt_ref[2 * side : 2 * side + 1, :] = keep_sorted.astype(F32)
        flt_ref[2 * side + 1 : 2 * side + 2, :] = jnp.minimum(here, 1).astype(F32)


def hand_on_kernel(*refs):
    half = len(refs) // 2
    for source, target in zip(refs[:half], refs[half:]):
        target[...] = source[...]


class Lines:
    def __init__(self, send_sems, recv_sems):
        self.send_sems, self.recv_sems, self.used, self.sent = send_sems, recv_sems, 0, []

    def line(self):
        self.used += 1
        return self.used - 1

    def send(self, line, src, dst, device):
        copy = pltpu.make_async_remote_copy(
            src_ref=src, dst_ref=dst, send_sem=self.send_sems.at[line], recv_sem=self.recv_sems.at[line],
            device_id=device, device_id_type=MESH)
        copy.start()
        self.sent.append(copy)

    def wait(self, line, dst, device):
        pltpu.make_async_remote_copy(
            src_ref=dst, dst_ref=dst, send_sem=self.send_sems.at[line], recv_sem=self.recv_sems.at[line],
            device_id=device, device_id_type=MESH).wait_recv()

    def drain(self):
        for copy in self.sent:
            copy.wait_send()


N_LINES = 160


def layer_kernel(
    count_ref, rows_hbm, cols_hbm, feat_hbm, weight_hbm, bias_hbm, cot_hbm, mask_hbm, adj_ref,
    out_hbm, gf_hbm, gw_hbm, gb_hbm,
    rows_ref, cols_ref, weight_ref, bias_ref, out_ref, gf_ref, gw_ref, gb_ref,
    idx_vmem, flt_vmem, idx_ref, flt_ref, cot_ref, mask_ref, adj, run, feats, proj, gpre, rsend, crecv, rown,
    zs1, zr1, zs2, zr2, zxs, zxr, ys1, yr1, ys2, yr2, yxs, yxr,
    agg, gsum, ar_col, ar_row, gall, bias_own, bias_col, bias_row,
    send_sems, recv_sems, in_sems):
    row, col = lax.axis_index("row"), lax.axis_index("col")
    xh, y = row // 4, row % 4
    xl, z, core = col // 8, (col // 2) % 4, col % 2
    lines = Lines(send_sems, recv_sems)

    def dev(xh=xh, y=y, xl=xl, z=z, core=core):
        return (xh * 4 + y, (xl * 4 + z) * 2 + core)

    def at_y(step):
        return dev(y=(y + step) % 4)

    def at_z(step):
        return dev(z=(z + step) % 4)

    pair_x = dev(xh=1 - xh)
    near_x = dev(xl=1 - xl)
    other = dev(core=1 - core)
    col_mates, row_mates = [], []
    for flip in (1, 0):
        for step in (2, 1, 3, 0):
            for turn in (1, 0):
                if flip or step or turn:
                    to_xl, to_z, to_core = (xl + flip) % 2, (z + step) % 4, (core + turn) % 2
                    col_mates.append((dev(xl=to_xl, z=to_z, core=to_core), (to_xl * 4 + to_z) * 2 + to_core))
            if flip or step:
                to_xh, to_y = (xh + flip) % 2, (y + step) % 4
                row_mates.append((dev(xh=to_xh, y=to_y), to_xh * 4 + to_y))
    partners = [mate for mate, _ in row_mates + col_mates]
    feat_copy = pltpu.make_async_copy(feat_hbm, feats.at[pl.ds(row * SHARD, SHARD)], in_sems.at[5])
    weight_copy = pltpu.make_async_copy(weight_hbm, weight_ref, in_sems.at[6])
    cot_copy = pltpu.make_async_copy(cot_hbm, cot_ref, in_sems.at[0])
    mask_copy = pltpu.make_async_copy(mask_hbm, mask_ref, in_sems.at[1])
    rows_copy = pltpu.make_async_copy(rows_hbm, rows_ref, in_sems.at[8])
    cols_copy = pltpu.make_async_copy(cols_hbm, cols_ref, in_sems.at[9])
    bias_copy = pltpu.make_async_copy(bias_hbm, bias_ref, in_sems.at[7])
    adj_copy = pltpu.make_async_copy(adj_ref, adj, in_sems.at[2])

    barrier = pltpu.get_barrier_semaphore()
    for partner in partners:
        pl.semaphore_signal(barrier, inc=1, device_id=partner, device_id_type=MESH)
    for copy in (cot_copy, mask_copy, weight_copy, feat_copy, rows_copy, cols_copy, bias_copy, adj_copy):
        copy.start()

    gb_ref[...] = jnp.zeros_like(gb_ref)
    weight_copy.wait()
    cot_copy.wait()
    mask_copy.wait()

    def project(b, _):
        nodes = pl.ds(pl.multiple_of(b * BLK, BLK), BLK)
        grad = cot_ref[nodes, :].astype(F32) * mask_ref[nodes, :].astype(F32)
        grad16 = grad.astype(BF16)
        gpre[nodes, :] = grad16
        gb_ref[...] += jnp.sum(grad16.astype(F32), axis=0, keepdims=True)
        turned = lax.dot_general(weight_ref[...], grad16, (((1,), (1,)), ((), ())), preferred_element_type=F32)
        proj[col * SHARD + b] = turned.astype(BF16)
        return 0

    lax.fori_loop(0, SHARD, project, 0, unroll=SHARD)
    pl.semaphore_wait(barrier, len(partners))

    def part(buf, shard, half):
        return buf.at[pl.ds(shard * SHARD + half * HALF, HALF)]

    class Gather:
        def __init__(self, buf, own, shard, pos, pair, ring, mate):
            self.buf, self.own, self.shard, self.pos, self.pair, self.ring, self.mate = buf, own, shard, pos, pair, ring, mate
            self.l0 = [lines.line() for _ in range(2)]
            self.l1 = [[lines.line() for _ in range(2)] for _ in range(2)]
            self.l2 = [lines.line() for _ in range(2)]
            self.l3 = [[lines.line() for _ in range(2)] for _ in range(2)]
            self.l4 = [lines.line() for _ in range(2)]
            self.lf = lines.line()

        def place(self, pair_step, step, half):
            pair = self.pair if pair_step == 0 else 1 - self.pair
            return part(self.buf, self.shard(pair, (self.pos + step) % 4), half)

        def begin(self):
            for half in range(2):
                for d in range(2):
                    h = half if d == 0 else 1 - half
                    lines.send(self.l1[d][h], self.own(h), self.place(0, 0, h), self.ring(1 - 2 * d))
                lines.send(self.l0[half], self.own(half), self.place(0, 0, half), self.mate)

        def got_mate(self, h):
            lines.wait(self.l0[h], self.place(1, 0, h), self.mate)
            return self.place(1, 0, h)

        def pass_mate(self, h):
            for d in range(2):
                lines.send(self.l3[d][h], self.place(1, 0, h), self.place(1, 0, h), self.ring(1 - 2 * d))

        def got_ring(self, kind, d, h):
            step = 2 * d - 1
            table = self.l1 if kind == 0 else self.l3
            place = self.place(kind, step, h)
            lines.wait(table[d][h], place, self.ring(step))
            return place

        def pass_ring(self, kind, d):
            step = 2 * d - 1
            table = self.l2 if kind == 0 else self.l4
            place = self.place(kind, step, d)
            lines.send(table[d], place, place, self.ring(-step))

        def quarter(self, step, d):
            shard = self.shard(1 - self.pair, (self.pos + step) % 4)
            return self.buf.at[pl.ds(shard * SHARD + d * (HALF // 2), HALF // 2)]

        def pass_quarter(self, d):
            place = self.quarter(2 * d - 1, d)
            lines.send(self.l4[d], place, place, self.ring(1 - 2 * d))

        def got_quarter(self, d):
            lines.wait(self.l4[d], self.quarter(2, d), self.ring(2 * d - 1))

        def far_to_mate(self):
            place = self.place(0, 2, 1)
            lines.send(self.lf, place, place, self.mate)

        def far_from_mate(self):
            lines.wait(self.lf, self.place(1, 2, 1), self.mate)

        def got_far(self, kind, d):
            step = 2 * d - 1
            table = self.l2 if kind == 0 else self.l4
            place = self.place(kind, 2, d)
            lines.wait(table[d], place, self.ring(step))
            return place

    feat_copy.wait()
    rows_g = Gather(feats, lambda h: part(feats, row, h),
                    lambda pair, pos: pair * 4 + pos, y, xh, at_y, pair_x)
    rows_g.begin()

    cols_g = Gather(proj, lambda h: part(proj, col, h),
                    lambda pair, pos: (pair * 4 + pos) * 2 + core, z, xl, at_z, near_x)
    cols_g.begin()

    across = []

    def cross(pair_step, step, h):
        line = lines.line()
        place = cols_g.place(pair_step, step, h)
        lines.send(line, place, place, other)
        pair = xl if pair_step == 0 else 1 - xl
        there = part(proj, (pair * 4 + (z + step) % 4) * 2 + 1 - core, h)
        across.append((line, there))

    cross(0, 0, 0)
    cross(0, 0, 1)
    for copy in (rows_copy, cols_copy, bias_copy):
        copy.wait()
    plan(count_ref, rows_ref, cols_ref, idx_vmem, flt_vmem)
    idx_copy = pltpu.make_async_copy(idx_vmem, idx_ref, in_sems.at[3])
    flt_copy = pltpu.make_async_copy(flt_vmem, flt_ref, in_sems.at[4])
    idx_copy.start()
    flt_copy.start()
    for d in range(2):
        rows_g.got_ring(0, d, d)
        rows_g.pass_ring(0, d)
    for d in range(2):
        cols_g.got_ring(0, d, d)
        cols_g.pass_ring(0, d)
    for h in range(2):
        rows_g.got_mate(h)
    for h in range(2):
        rows_g.pass_mate(h)
    for d in (1, 0):
        rows_g.got_far(0, d)
        if d == 1:
            rows_g.far_to_mate()
    for h in range(2):
        cols_g.got_mate(h)
        cols_g.pass_mate(h)
    for d in range(2):
        cross(0, 2 * d - 1, d)
        cross(1, 0, d)
    for d in range(2):
        cols_g.got_ring(0, d, 1 - d)
        cross(0, 2 * d - 1, 1 - d)
    for d in range(2):
        rows_g.got_ring(1, d, 0)
        rows_g.pass_quarter(d)
    for d in range(2):
        cols_g.got_far(0, d)
        cross(0, 2, d)
    for d in range(2):
        cols_g.got_ring(1, d, d)
        cols_g.pass_ring(1, d)
        cross(1, 2 * d - 1, d)
    for d in range(2):
        rows_g.got_ring(0, d, 1 - d)
        rows_g.got_ring(1, d, 1)
    for d in range(2):
        rows_g.got_quarter(d)
    rows_g.far_from_mate()
    adj_copy.wait()
    idx_copy.wait()
    flt_copy.wait()

    def spread(mates, source, target, place):
        used = [lines.line() for _ in mates]
        for line, (mate, theirs) in zip(used, mates):
            lines.send(line, source(theirs), target.at[place], mate)
        return used

    def collect(mates, used, target):
        for line, (mate, theirs) in zip(used, mates):
            lines.wait(line, target.at[theirs], mate)

    def added(ref):
        total = ref[0]
        for n in range(1, ref.shape[0]):
            total = total + ref[n]
        return total

    bias_own[0] = gb_ref[...]
    bias_col[col] = gb_ref[...]
    bias_lines = spread(col_mates, lambda theirs: bias_own.at[0], bias_col, col)

    slots = adj.shape[0]

    def forward(p, total):
        total = total * flt_ref[0, p] + jnp.dot(adj[idx_ref[0, p]], feats[idx_ref[1, p]], preferred_element_type=F32)
        run[p] = total
        return total

    lax.fori_loop(0, slots, forward, jnp.zeros((BLK, BLK), F32), unroll=128)

    def row_block(b):
        return run[idx_ref[2, b]] * flt_ref[1, b]

    order = [(1, 2), (1, 1), (1, -1), (0, 1), (0, -1), (0, 2), (1, 0), (0, 0)]

    def spot(pair, pos, step):
        return pair * 4 + (pos + step) % 4

    core_lines = {}
    for pair_step, step in order:
        q = spot(1 - xl if pair_step else xl, z, step)

        def fill(b, _, q=q):
            rsend[q * SHARD + b] = row_block((q * 2 + 1 - core) * SHARD + b).astype(BF16)
            return 0

        lax.fori_loop(0, SHARD, fill, 0, unroll=SHARD)
        line = core_lines[pair_step, step] = lines.line()
        place = pl.ds(q * SHARD, SHARD)
        lines.send(line, rsend.at[place], crecv.at[place], other)

    def add_core(pair_step, step):
        q = spot(1 - xl if pair_step else xl, z, step)
        lines.wait(core_lines[pair_step, step], crecv.at[pl.ds(q * SHARD, SHARD)], other)

        def fill(b, _):
            rown[q * SHARD + b] = row_block((q * 2 + core) * SHARD + b) + crecv[q * SHARD + b].astype(F32)
            return 0

        lax.fori_loop(0, SHARD, fill, 0, unroll=SHARD)

    class Scatter:
        def __init__(self, s1, r1, s2, r2, xs, xr, term, ring, mate, far_by_mate):
            self.s1, self.r1, self.s2, self.r2, self.xs, self.xr = s1, r1, s2, r2, xs, xr
            self.term, self.ring, self.mate, self.far_by_mate = term, ring, mate, far_by_mate
            self.l1 = [[lines.line() for _ in range(2)] for _ in range(2)]
            self.l2 = [[[lines.line() for _ in range(2)] for _ in range(2)] for _ in range(2)]
            self.l2b = [lines.line() for _ in range(2)]
            self.lx = [lines.line() for _ in range(2)]

        def far(self, pair_step, ways=(0, 1)):
            for d in ways:
                if self.far_by_mate and pair_step == 0:
                    lines.wait(self.l1[1][d], self.r1.at[pl.ds(SHARD + d * HALF, HALF)], self.mate)

                def fill(b, _, d=d):
                    b = d * HALF + b
                    value = self.term(pair_step, 2, b)
                    if self.far_by_mate and pair_step == 0:
                        value = value + self.r1[SHARD + b].astype(F32)
                    self.s1[pair_step * SHARD + b] = value.astype(BF16)
                    return 0

                lax.fori_loop(0, HALF, fill, 0, unroll=HALF)
                place = pl.ds(pair_step * SHARD + d * HALF, HALF)
                lines.send(self.l1[pair_step][d], self.s1.at[place], self.r1.at[place],
                           self.mate if self.far_by_mate and pair_step else self.ring(1 - 2 * d))

        def near(self, pair_step, d, late, cut=None):
            h = d if late else 1 - d
            first = h * HALF + (cut or 0) * (HALF // 2)
            count = HALF if cut is None else HALF // 2
            base = (pair_step * 2 + d) * SHARD + first
            line = self.l2b[d] if cut else self.l2[pair_step][d][h]
            passing = late and not (self.far_by_mate and pair_step)
            if passing:
                place = pl.ds(pair_step * SHARD + d * HALF, HALF)
                lines.wait(self.l1[pair_step][d], self.r1.at[place], self.ring(2 * d - 1))

            def fill(b, _):
                value = self.term(pair_step, 1 - 2 * d, first + b)
                if passing:
                    value = value + self.r1[pair_step * SHARD + d * HALF + b].astype(F32)
                self.s2[base + b] = value.astype(BF16)
                return 0

            lax.fori_loop(0, count, fill, 0, unroll=count)
            place = pl.ds(base, count)
            lines.send(line, self.s2.at[place], self.r2.at[place], self.ring(1 - 2 * d))

        def wait_near(self, pair_step, h):
            for d in range(2):
                base = (pair_step * 2 + d) * SHARD + h * HALF
                if pair_step == 0 and h == 1 - d:
                    for cut, line in enumerate((self.l2[0][d][h], self.l2b[d])):
                        lines.wait(line, self.r2.at[pl.ds(base + cut * (HALF // 2), HALF // 2)], self.ring(2 * d - 1))
                else:
                    lines.wait(self.l2[pair_step][d][h], self.r2.at[pl.ds(base, HALF)], self.ring(2 * d - 1))

        def total(self, pair_step, b):
            base = pair_step * 2 * SHARD + b
            return (self.term(pair_step, 0, b) + self.r2[base].astype(F32)) + self.r2[base + SHARD].astype(F32)

        def swap(self, h):
            self.wait_near(1, h)

            def fill(b, _):
                self.xs[h * HALF + b] = self.total(1, h * HALF + b).astype(BF16)
                return 0

            lax.fori_loop(0, HALF, fill, 0, unroll=HALF)
            place = pl.ds(h * HALF, HALF)
            lines.send(self.lx[h], self.xs.at[place], self.xr.at[place], self.mate)

        def finish(self, h, use):
            self.wait_near(0, h)
            lines.wait(self.lx[h], self.xr.at[pl.ds(h * HALF, HALF)], self.mate)

            def body(b, _):
                b = h * HALF + b
                use(b, self.total(0, b) + self.xr[b].astype(F32))
                return 0

            lax.fori_loop(0, HALF, body, 0, unroll=HALF)

    def row_term(pair_step, step, b):
        return rown[spot(1 - xl if pair_step else xl, z, step) * SHARD + b]

    rows_s = Scatter(zs1, zr1, zs2, zr2, zxs, zxr, row_term, at_z, near_x, True)
    add_core(1, 2)
    rows_s.far(1)
    for d in range(2):
        add_core(1, 1 - 2 * d)
        rows_s.near(1, d, False)
    for d in range(2):
        rows_s.near(1, d, True)
    for d in range(2):
        add_core(0, 1 - 2 * d)
        rows_s.near(0, d, False, 0)
    add_core(0, 2)
    for pair_step in (1, 0):
        add_core(pair_step, 0)
    for d in range(2):
        cols_g.got_ring(1, d, 1 - d)
        cross(1, 2 * d - 1, 1 - d)
    for d in range(2):
        cols_g.got_far(1, d)
        cross(1, 2, d)

    for line, there in across:
        lines.wait(line, there, other)

    def backward(p, total):
        total = total * flt_ref[2, p] + jnp.dot(proj[idx_ref[4, p]], adj[idx_ref[3, p]], preferred_element_type=F32)
        run[p] = total
        return total

    lax.fori_loop(0, slots, backward, jnp.zeros((BLK, BLK), F32), unroll=32)

    def col_term(pair_step, step, b):
        at = spot(1 - xh if pair_step else xh, y, step) * SHARD + b
        return run[idx_ref[5, at]] * flt_ref[3, at]

    cols_s = Scatter(ys1, yr1, ys2, yr2, yxs, yxr, col_term, at_y, pair_x, False)
    cols_s.far(1)
    for d in range(2):
        cols_s.near(1, d, False)
    for d in range(2):
        rows_s.far(0, (d,))
        rows_s.near(0, d, False, 1)
    for h in range(2):
        rows_s.swap(h)
    for d in range(2):
        cols_s.near(1, d, True)
    cols_s.far(0)
    for d in range(2):
        for cut in range(2):
            cols_s.near(0, d, False, cut)
    for d in range(2):
        rows_s.near(0, d, True)

    def aggregate(b, value):
        agg[b] = value.astype(BF16)

    def layer(b, _):
        nodes = pl.ds(pl.multiple_of(b * BLK, BLK), BLK)
        pre = jnp.dot(agg[b], weight_ref[...], preferred_element_type=F32) + bias_ref[...]
        out_ref[nodes, :] = (pre * mask_ref[nodes, :].astype(F32)).astype(BF16)
        return 0

    for h in range(2):
        rows_s.finish(h, aggregate)

    def weight_term(b, total):
        nodes = pl.ds(pl.multiple_of(b * BLK, BLK), BLK)
        return total + lax.dot_general(agg[b], gpre[nodes, :], (((0,), (0,)), ((), ())), preferred_element_type=F32)

    gw_ref[...] = lax.fori_loop(0, SHARD, weight_term, jnp.zeros(gw_ref.shape, F32), unroll=SHARD)

    pieces, depth = gsum.shape[0], gsum.shape[1]
    for n in range(pieces):
        gsum[n] = gw_ref[pl.ds(n * depth, depth), :]
    used = spread(col_mates, lambda theirs: gsum.at[theirs], ar_col, col)
    ar_col[col] = gsum[col]
    collect(col_mates, bias_lines, bias_col)
    bias_row[row] = added(bias_col)
    bias_lines = spread(row_mates, lambda theirs: bias_row.at[row], bias_row, row)
    lax.fori_loop(0, SHARD, layer, 0, unroll=SHARD)
    out_copy = pltpu.make_async_copy(out_ref, out_hbm, in_sems.at[10])
    out_copy.start()
    for h in range(2):
        cols_s.swap(h)
    for d in range(2):
        cols_s.near(0, d, True)
    collect(col_mates, used, ar_col)
    ar_row[row] = added(ar_col)
    used = spread(row_mates, lambda theirs: ar_row.at[row], ar_row, row)
    collect(row_mates, used, ar_row)
    gall[col] = added(ar_row)
    used = spread(col_mates, lambda theirs: gall.at[col], gall, col)

    def store(b, value):
        gf_ref[b] = jnp.transpose(value).astype(BF16)

    for h in range(2):
        cols_s.finish(h, store)
    gf_copy = pltpu.make_async_copy(gf_ref, gf_hbm, in_sems.at[11])
    gf_copy.start()

    collect(row_mates, bias_lines, bias_row)
    gb_ref[...] = added(bias_row)
    collect(col_mates, used, gall)
    for n in range(pieces):
        gw_ref[pl.ds(n * depth, depth), :] = gall[n]
    gw_copy = pltpu.make_async_copy(gw_ref, gw_hbm, in_sems.at[12])
    gb_copy = pltpu.make_async_copy(gb_ref, gb_hbm, in_sems.at[13])
    gw_copy.start()
    gb_copy.start()
    lines.drain()
    for copy in (out_copy, gf_copy, gw_copy, gb_copy):
        copy.wait()
    assert lines.used <= N_LINES


def local(features, weight, bias, adjacency, block_rows, block_cols, block_count, cotangent, relu_mask):
    slots = adjacency.shape[2]
    vmem, smem, hbm = (pl.BlockSpec(memory_space=m) for m in (pltpu.VMEM, pltpu.SMEM, pl.ANY))
    hid = weight.shape[1]

    def blocks(n, dtype=BF16):
        return pltpu.VMEM((n, BLK, BLK), dtype)

    plan_shape = (8, slots)
    scratch = [
        pltpu.VMEM((1, slots), jnp.int32), pltpu.VMEM((1, slots), jnp.int32), pltpu.VMEM(weight.shape, BF16), pltpu.VMEM((1, hid), F32),
        pltpu.VMEM((1024, hid), BF16), pltpu.VMEM((SHARD, BLK, BLK), BF16), pltpu.VMEM(weight.shape, F32), pltpu.VMEM((1, hid), F32),
        pltpu.VMEM(plan_shape, jnp.int32), pltpu.VMEM(plan_shape, F32), pltpu.SMEM(plan_shape, jnp.int32), pltpu.SMEM(plan_shape, F32),
        pltpu.VMEM((1024, hid), BF16), pltpu.VMEM((1024, hid), jnp.int32),
        blocks(slots), blocks(slots, F32), blocks(64), blocks(128), pltpu.VMEM((1024, hid), BF16),
        blocks(64), blocks(64), blocks(64, F32)]
    for _ in range(2):
        scratch += [blocks(16), blocks(16), blocks(32), blocks(32), blocks(8), blocks(8)]
    piece = (8, hid)
    scratch += [blocks(8)] + [pltpu.VMEM((n,) + piece, F32) for n in (16, 16, 8, 16)]
    scratch += [pltpu.VMEM((n, 1, hid), F32) for n in (1, 16, 8)]
    scratch += [pltpu.SemaphoreType.DMA((N_LINES,)), pltpu.SemaphoreType.DMA((N_LINES,)), pltpu.SemaphoreType.DMA((14,))]
    out, gf, gw, gb = pl.pallas_call(
        layer_kernel,
        out_shape=(
            jax.ShapeDtypeStruct((1024, hid), BF16),
            jax.ShapeDtypeStruct((SHARD, BLK, BLK), BF16),
            jax.ShapeDtypeStruct(weight.shape, F32),
            jax.ShapeDtypeStruct((1, hid), F32),
        ),
        in_specs=[smem] + [hbm] * 8,
        out_specs=(hbm,) * 4,
        scratch_shapes=scratch,
        compiler_params=pltpu.CompilerParams(collective_id=0, has_side_effects=True, vmem_limit_bytes=60 * 2**20),
        name="layer",
    )(block_count, block_rows[0], block_cols[0], features.reshape(SHARD, BLK, BLK), weight, bias.reshape(1, hid), cotangent, relu_mask,
      adjacency.reshape(slots, BLK, BLK))
    results = (out, gf, gw, gb)
    out, gf, gw, gb = pl.pallas_call(
        hand_on_kernel,
        out_shape=tuple(jax.ShapeDtypeStruct(r.shape, r.dtype) for r in results),
        in_specs=[vmem] * 4,
        out_specs=(vmem,) * 4,
        name="hand_on",
    )(*results)
    return out, gf.reshape(1024, BLK), gw, gb.reshape(hid)


def solution(mesh):
    in_specs = (
        P(("col", "row"), None),
        P(),
        P(),
        P("row", "col", None, None, None),
        P("row", "col", None),
        P("row", "col", None),
        P("row", "col"),
        P(("row", "col"), None),
        P(("row", "col"), None),
    )
    out_specs = (P(("row", "col"), None), P(("col", "row"), None), P(), P())
    return jax.shard_map(local, mesh=mesh, in_specs=in_specs, out_specs=out_specs, check_vma=False)
```
